128 devices in a mesh: row: 8 (over y, x_hi), col: 16 (over z, x_lo, core).
Axes of the slice: x: 4 (x_hi: 2, x_lo: 2; x = x_hi * 2 + x_lo), y: 4, z: 4, core: 2. Of those that a mesh axis runs over, the one named last changes fastest.
Arguments:
- tokens: bfloat16 [128, 512, 256], P('row', 'col'), may hold values from -45 to 45
- cotangent: bfloat16 [128, 512, 256], P('row', 'col'), may hold values from -6 to 6
- gain_one: float32 [256], replicated, may hold values from 0.25 to 1.75
- qkv_weight: bfloat16 [256, 768], replicated, may hold values from -0.375 to 0.375
- proj_weight: bfloat16 [256, 256], replicated, may hold values from -0.375 to 0.375
- rel_bias: float32 [8, 64, 64], replicated, may hold values from -3 to 300
- gain_two: float32 [256], replicated, may hold values from 0.25 to 1.75
- fc_one: bfloat16 [256, 1024], replicated, may hold values from -0.375 to 0.375
- fc_two: bfloat16 [1024, 256], replicated, may hold values from -0.1875 to 0.1875
Outputs:
- output: bfloat16 [128, 512, 256], P('row', 'col')
- grad_tokens: bfloat16 [128, 512, 256], P('row', 'col')
- grad_qkv: float32 [256, 768], replicated
- grad_proj: float32 [256, 256], replicated
- grad_bias: float32 [8, 64, 64], replicated
- grad_fc_one: float32 [256, 1024], replicated
- grad_fc_two: float32 [1024, 256], replicated
- grad_gain_one: float32 [256], replicated
- grad_gain_two: float32 [256], replicated
The draws below stay inside these ranges and needn't reach their ends.
All inputs are finite; a program needn't handle non-finite values.
Results may differ from the reference program's by a relative error of at most 0.012.
The reference program's roundings to bfloat16 on the way count: a program that leaves them out, or rounds other values in their place, can miss the bound.
Values may be sent and summed in bfloat16 or wider, within the bound.
A program may use at most 128 MiB of HBM per device.

```python
import jax
import jax.numpy as jnp
from jax import lax

CHANNELS = 256
NUM_HEADS = 8
HEAD_DIM = 32
MLP_DIM = 1024
GRID_SIDE = 8
LATTICE_ROWS = 128
LATTICE_COLS = 512
TOKENS = 65536


def draw_tokens(key, part):
    key = jax.random.fold_in(key, 11)
    shape_all = (LATTICE_ROWS, LATTICE_COLS, CHANNELS)
    token_scale = jnp.exp(jax.random.uniform(jax.random.fold_in(key, 1), (LATTICE_ROWS, LATTICE_COLS, 1), jnp.float32, -1.2, 1.2))
    channel_scale = jnp.exp(jax.random.uniform(jax.random.fold_in(key, 2), (CHANNELS,), jnp.float32, -1.2, 1.2))
    base = jnp.clip(jax.random.normal(jax.random.fold_in(key, 4), shape_all, jnp.float32), -4.0, 4.0)
    return (base * token_scale * channel_scale).astype(jnp.bfloat16)


def draw_rel_bias(key, part):
    key = jax.random.fold_in(key, 23)
    grid_area = GRID_SIDE * GRID_SIDE
    shape_all = (NUM_HEADS, grid_area, grid_area)
    result = jnp.clip(jax.random.normal(jax.random.fold_in(key, 1), shape_all, jnp.float32), -3.0, 3.0)
    return result.astype(jnp.float32)


def levels(rng, shape, shards, least, top_value):
    def one(dim, parts):
        steps = jax.random.uniform(jax.random.fold_in(jax.random.fold_in(rng, 6), dim), (parts,), jnp.float32, least / len(shards), top_value / len(shards))
        return jnp.repeat(jnp.exp(steps), shape[dim] // parts).reshape((-1,) + (1,) * (len(shape) - dim - 1))

    loudness = one(*shards[0])
    for cut in shards[1:]:
        loudness = loudness * one(*cut)
    return loudness


def noise(rng, extent, width, bound, split=(), dtype=jnp.bfloat16):
    drawn = width * jax.random.normal(rng, extent, jnp.float32)
    if split:
        drawn = drawn * levels(rng, extent, split, -0.22, 0.18)
    return jnp.clip(drawn, -bound, bound).astype(dtype)


def setup_inputs(seed: int = 0) -> dict:
    key_of = jax.random.split(jax.random.key(seed), 10)
    return {
        "tokens": draw_tokens(jax.random.fold_in(key_of[9], 71), 0),
        "cotangent": noise(key_of[1], (LATTICE_ROWS, LATTICE_COLS, CHANNELS), 1.0, 6.0, ((0, 8), (1, 16))),
        "gain_one": jnp.clip(1.0 + 0.15 * jax.random.normal(key_of[2], (CHANNELS,), jnp.float32), 0.25, 1.75),
        "qkv_weight": noise(key_of[3], (CHANNELS, 3 * CHANNELS), CHANNELS ** -0.5, 0.375),
        "proj_weight": noise(key_of[4], (CHANNELS, CHANNELS), CHANNELS ** -0.5, 0.375),
        "rel_bias": draw_rel_bias(jax.random.fold_in(key_of[9], 71), 0),
        "gain_two": jnp.clip(1.0 + 0.15 * jax.random.normal(key_of[6], (CHANNELS,), jnp.float32), 0.25, 1.75),
        "fc_one": noise(key_of[7], (CHANNELS, MLP_DIM), CHANNELS ** -0.5, 0.375),
        "fc_two": noise(key_of[8], (MLP_DIM, CHANNELS), MLP_DIM ** -0.5, 0.1875),
    }


EPSILON = 1e-05
ROOT_HALF = 0.7071067811865476
DENSITY = 0.3989422804014327

def rounded(values):
    return lax.optimization_barrier(values.astype(jnp.bfloat16))

def norm_forward(values):
    centre = lax.optimization_barrier(jnp.mean(values, axis=-1, keepdims=True))
    shifted = values - centre
    spread = lax.optimization_barrier(jnp.mean(shifted * shifted, axis=-1, keepdims=True))
    inverse = lax.rsqrt(spread + EPSILON)
    return (shifted * inverse, inverse)

def norm_backward(upstream, normed, inverse, gain_vec):
    scaled = upstream * gain_vec
    mean_first = lax.optimization_barrier(jnp.mean(scaled, axis=-1, keepdims=True))
    second = lax.optimization_barrier(jnp.mean(scaled * normed, axis=-1, keepdims=True))
    return inverse * (scaled - mean_first - normed * second)

def gelu_parts(preact):
    normal_cdf = 0.5 * (1.0 + lax.erf(preact * ROOT_HALF))
    return (preact * normal_cdf, normal_cdf + preact * DENSITY * jnp.exp(-0.5 * preact * preact))

def window_pass(tokens_win, cotangent_win, gain_one, qkv_weight, proj_weight, rel_bias, gain_two, fc_one, fc_two):
    window_count = tokens_win.shape[0]
    grid_area = GRID_SIDE * GRID_SIDE
    score_scale = HEAD_DIM ** (-0.5)
    tokens_flat = tokens_win.reshape(-1, CHANNELS).astype(jnp.float32)
    normed_one, inverse_one = norm_forward(tokens_flat)
    normed_in = rounded(normed_one * gain_one)
    projected = rounded(jnp.dot(normed_in, qkv_weight, preferred_element_type=jnp.float32))
    projected = projected.reshape(window_count, grid_area, 3, NUM_HEADS, HEAD_DIM).astype(jnp.float32)
    queries = projected[:, :, 0]
    keys_part = projected[:, :, 1]
    values_part = projected[:, :, 2]
    scores = jnp.einsum('wphd,wqhd->whpq', queries, keys_part) * score_scale + rel_bias
    score_probs = jax.nn.softmax(scores, axis=-1)
    probs_low = rounded(score_probs).astype(jnp.float32)
    attended = rounded(jnp.einsum('whpq,wqhd->wphd', probs_low, values_part)).reshape(-1, CHANNELS)
    branch = rounded(jnp.dot(attended, proj_weight, preferred_element_type=jnp.float32))
    middle = rounded(tokens_flat + branch.astype(jnp.float32))
    middle_f = middle.astype(jnp.float32)
    normed_two, inverse_two = norm_forward(middle_f)
    normed_mid = rounded(normed_two * gain_two)
    preact = jnp.dot(normed_mid, fc_one, preferred_element_type=jnp.float32)
    activation, gelu_slope = gelu_parts(preact)
    activation_low = rounded(activation)
    output = rounded(middle_f + jnp.dot(activation_low, fc_two, preferred_element_type=jnp.float32))
    upstream = cotangent_win.reshape(-1, CHANNELS)
    grad_fc_two = jnp.dot(activation_low.T, upstream, preferred_element_type=jnp.float32)
    grad_act = jnp.dot(upstream, fc_two.T, preferred_element_type=jnp.float32)
    grad_pre = rounded(grad_act * gelu_slope)
    grad_fc_one = jnp.dot(normed_mid.T, grad_pre, preferred_element_type=jnp.float32)
    grad_norm_mid = jnp.dot(grad_pre, fc_one.T, preferred_element_type=jnp.float32)
    grad_gain_two = lax.optimization_barrier(jnp.sum(grad_norm_mid * normed_two, axis=0))
    grad_middle = rounded(upstream.astype(jnp.float32) + norm_backward(grad_norm_mid, normed_two, inverse_two, gain_two))
    grad_proj = jnp.dot(attended.T, grad_middle, preferred_element_type=jnp.float32)
    grad_att = rounded(jnp.dot(grad_middle, proj_weight.T, preferred_element_type=jnp.float32))
    grad_att = grad_att.reshape(window_count, grid_area, NUM_HEADS, HEAD_DIM).astype(jnp.float32)
    grad_probs = jnp.einsum('wphd,wqhd->whpq', grad_att, values_part)
    grad_values = jnp.einsum('whpq,wphd->wqhd', probs_low, grad_att)
    grad_scores = score_probs * (grad_probs - lax.optimization_barrier(jnp.sum(score_probs * grad_probs, axis=-1, keepdims=True)))
    grad_bias = lax.optimization_barrier(jnp.sum(grad_scores, axis=0))
    scores_low = rounded(grad_scores).astype(jnp.float32)
    grad_queries = jnp.einsum('whpq,wqhd->wphd', scores_low, keys_part) * score_scale
    grad_keys = jnp.einsum('whpq,wphd->wqhd', scores_low, queries) * score_scale
    grad_projected = rounded(jnp.stack([grad_queries, grad_keys, grad_values], axis=2)).reshape(-1, 3 * CHANNELS)
    grad_qkv = jnp.dot(normed_in.T, grad_projected, preferred_element_type=jnp.float32)
    grad_normed_in = rounded(jnp.dot(grad_projected, qkv_weight.T, preferred_element_type=jnp.float32)).astype(jnp.float32)
    grad_gain_one = lax.optimization_barrier(jnp.sum(grad_normed_in * normed_one, axis=0))
    grad_tokens = rounded(grad_middle.astype(jnp.float32) + norm_backward(grad_normed_in, normed_one, inverse_one, gain_one))
    shape_win = (window_count, GRID_SIDE, GRID_SIDE, CHANNELS)
    return ((output.reshape(shape_win), grad_tokens.reshape(shape_win)), (grad_qkv, grad_proj, grad_bias, grad_fc_one, grad_fc_two, grad_gain_one, grad_gain_two))

def reference(tokens, cotangent, gain_one, qkv_weight, proj_weight, rel_bias, gain_two, fc_one, fc_two):
    block_rows = LATTICE_ROWS // GRID_SIDE
    block_cols = LATTICE_COLS // GRID_SIDE
    grid_area = GRID_SIDE * GRID_SIDE

    def to_grid(lattice):
        return jnp.transpose(lattice.reshape(GRID_SIDE, block_rows, GRID_SIDE, block_cols, CHANNELS), (1, 3, 0, 2, 4))

    def from_grid(windows):
        return jnp.transpose(windows, (2, 0, 3, 1, 4)).reshape(LATTICE_ROWS, LATTICE_COLS, CHANNELS)
    initial = (jnp.zeros((CHANNELS, 3 * CHANNELS), jnp.float32), jnp.zeros((CHANNELS, CHANNELS), jnp.float32), jnp.zeros((NUM_HEADS, grid_area, grid_area), jnp.float32), jnp.zeros((CHANNELS, MLP_DIM), jnp.float32), jnp.zeros((MLP_DIM, CHANNELS), jnp.float32), jnp.zeros((CHANNELS,), jnp.float32), jnp.zeros((CHANNELS,), jnp.float32))

    def window_step(totals, inputs):
        results, grads = window_pass(inputs[0], inputs[1], gain_one, qkv_weight, proj_weight, rel_bias, gain_two, fc_one, fc_two)
        return (tuple((total + piece for total, piece in zip(totals, grads))), results)
    totals, results = lax.scan(window_step, initial, (to_grid(tokens), to_grid(cotangent)))
    grad_scale = TOKENS ** (-0.5)
    grad_qkv, grad_proj, grad_bias, grad_fc_one, grad_fc_two, grad_gain_one, grad_gain_two = totals
    return (from_grid(results[0]), from_grid(results[1]), grad_qkv * grad_scale, grad_proj * grad_scale, grad_bias * (grad_scale * GRID_SIDE * GRID_SIDE), grad_fc_one * grad_scale, grad_fc_two * grad_scale, grad_gain_one * grad_scale, grad_gain_two * grad_scale)
```

```python
import functools

import jax
import jax.numpy as jnp
from jax import lax
from jax.experimental import pallas as pl
from jax.experimental.pallas import tpu as pltpu
from jax.sharding import PartitionSpec as P

NUM_HEADS = 8
HEAD_DIM = 32
GRID_SIDE = 8
AREA = GRID_SIDE * GRID_SIDE
CHANNELS = 256
MLP_DIM = 1024
WINDOWS = 8
LOCAL = WINDOWS * AREA
PAIRS = 4
LANES = 128
PIECES = 16

EPSILON = 1e-05
ROOT_HALF = 0.7071067811865476
DENSITY = 0.3989422804014327
SCORE_SCALE = HEAD_DIM ** (-0.5)

MESH = pl.DeviceIdType.MESH
BF16 = jnp.bfloat16
F32 = jnp.float32


def low(values):
    return values.astype(BF16)


def wide(values):
    return values.astype(F32)


def dot_nn(a, b):
    return lax.dot_general(a, b, (((1,), (0,)), ((), ())), preferred_element_type=F32)


def dot_nt(a, b):
    return lax.dot_general(a, b, (((1,), (1,)), ((), ())), preferred_element_type=F32)


def dot_tn(a, b):
    return lax.dot_general(a, b, (((0,), (0,)), ((), ())), preferred_element_type=F32)


def norm_forward(values):
    centre = jnp.mean(values, axis=-1, keepdims=True)
    shifted = values - centre
    spread = jnp.mean(shifted * shifted, axis=-1, keepdims=True)
    inverse = lax.rsqrt(spread + EPSILON)
    return (shifted * inverse, inverse)


def norm_backward(upstream, normed, inverse, gain_vec):
    scaled = upstream * gain_vec
    mean_first = jnp.mean(scaled, axis=-1, keepdims=True)
    second = jnp.mean(scaled * normed, axis=-1, keepdims=True)
    return inverse * (scaled - mean_first - normed * second)


def gelu_parts(preact):
    normal_cdf = 0.5 * (1.0 + lax.erf(preact * ROOT_HALF))
    return (preact * normal_cdf, normal_cdf + preact * DENSITY * jnp.exp(-0.5 * preact * preact))


def device_at(x, y, z, core):
    return (y * 2 + x // 2, (z * 2 + x % 2) * 2 + core)


def pack_tile(tile):
    return low(jnp.concatenate([tile[:, :, :LANES], tile[:, :, LANES:]], axis=1))


def fused_kernel(
    tokens_ref, cot_ref, gain_one_ref, wqkv_ref, wproj_ref, bias_ref, gain_two_ref, fc1_ref, fc2_ref,
    out_back, grad_back, gath_a, gath_b, gath_c,
    tok_send, cot_send, out_send, grad_send, tok_recv, cot_recv,
    part_a, part_b, part_c, crecv_a, crecv_b, crecv_c, psend_a, psend_b, psend_c,
    precv_a, precv_b, precv_c, axis_a, axis_b, axis_c,
    mix, x_ref, cot_w, cot_low, n1_ref, n1_low, qkv_ref, att_ref, n2_ref, n2_low, mid_ref,
    acc_ref, gnm_ref, gm_low, gatt_ref, gp_ref, bias_t, gbias, probs_ref, kbig_ref, vbig_ref,
    sems,
):
    row, col = lax.axis_index("row"), lax.axis_index("col")
    core = col % 2
    me = row * GRID_SIDE + col // 2
    x, y, z = (row % 2) * 2 + (col // 2) % 2, row // 2, col // 4
    partner = (row, col + 1 - 2 * core)

    def chip(p):
        return (p // GRID_SIDE, (p % GRID_SIDE) * 2 + core)

    barrier = pltpu.get_barrier_semaphore()

    def greet(i, carry):
        pl.semaphore_signal(barrier, inc=1, device_id=chip(lax.rem(me + i, AREA)), device_id_type=MESH)
        return carry

    lax.fori_loop(1, AREA, greet, 0)
    pl.semaphore_signal(barrier, inc=1, device_id=partner, device_id_type=MESH)

    def exchange_start(send, recv, k):
        def step(i, carry):
            p = lax.rem(me + i, AREA)
            pltpu.make_async_remote_copy(
                src_ref=send.at[p], dst_ref=recv.at[me], send_sem=sems.at[2 * k], recv_sem=sems.at[2 * k + 1],
                device_id=chip(p), device_id_type=MESH,
            ).start()
            return carry

        lax.fori_loop(1, AREA, step, 0)
        recv[me] = send[me]

    def drain(ref, sem):
        pltpu.make_async_copy(ref, ref, sem).wait()

    def exchange_recv(recv, k):
        drain(recv.at[pl.ds(0, AREA - 1)], sems.at[2 * k + 1])

    def exchange_sent(send, k):
        drain(send.at[pl.ds(0, AREA - 1)], sems.at[2 * k])

    def device_a(j):
        return device_at(x, j // 4, j % 4, core)

    def device_b(j):
        return device_at(j % 4, y, j // 4, core)

    def device_c(j):
        return device_at(j % 4, j // 4, z, core)

    parts = (
        (part_a, crecv_a, psend_a, precv_a, axis_a, gath_a, device_a, y * 4 + z,
         lambda t: device_at(t, y, z, core), x, 8),
        (part_b, crecv_b, psend_b, precv_b, axis_b, gath_b, device_b, z * 4 + x,
         lambda t: device_at(x, t, z, core), y, 18),
        (part_c, crecv_c, psend_c, precv_c, axis_c, gath_c, device_c, y * 4 + x,
         lambda t: device_at(x, y, t, core), z, 28),
    )

    def remote(src, dst, k, device):
        return pltpu.make_async_remote_copy(
            src_ref=src, dst_ref=dst, send_sem=sems.at[k], recv_sem=sems.at[k + 1],
            device_id=device, device_id_type=MESH,
        )

    def core_start(g):
        part, crecv, k = g[0], g[1], g[10]
        remote(part.at[1 - core], crecv, k, partner).start()

    def plane_start(g):
        part, crecv, psend, precv, where, mine, k = g[0], g[1], g[2], g[3], g[6], g[7], g[10]
        remote(part.at[1 - core], crecv, k, partner).wait()
        psend[...] = low(wide(part[core]) + wide(crecv[...]))

        def step(i, carry):
            j = lax.rem(mine + i, PIECES)
            remote(psend.at[j], precv.at[mine], k + 2, where(j)).start()
            return carry

        lax.fori_loop(1, PIECES, step, 0)
        precv[mine] = psend[mine]

    def axis_start(g):
        psend, precv, axis, along, place, k = g[2], g[3], g[4], g[8], g[9], g[10]
        drain(psend.at[pl.ds(0, PIECES - 1)], sems.at[k + 2])
        drain(precv.at[pl.ds(0, PIECES - 1)], sems.at[k + 3])
        axis[place] = low(jnp.sum(wide(precv[...]), axis=0))
        for i in range(1, 4):
            remote(axis.at[place], axis.at[place], k + 4, along(lax.rem(place + i, 4))).start()

    def gather_start(g):
        axis, gath, where, mine, k = g[4], g[5], g[6], g[7], g[10]
        drain(axis.at[pl.ds(0, 3)], sems.at[k + 4])
        drain(axis.at[pl.ds(0, 3)], sems.at[k + 5])
        gath[core, mine] = low(jnp.sum(wide(axis[...]), axis=0))

        def step(i, carry):
            j = lax.rem(mine + i, PIECES)
            remote(gath.at[core, mine], gath.at[core, mine], k + 6, where(j)).start()
            return carry

        lax.fori_loop(1, PIECES, step, 0)

    def share_start(g):
        gath, k = g[5], g[10]
        drain(gath.at[core, pl.ds(0, PIECES - 1)], sems.at[k + 6])
        drain(gath.at[core, pl.ds(0, PIECES - 1)], sems.at[k + 7])
        remote(gath.at[core], gath.at[core], k + 8, partner).start()

    def share_wait(g):
        gath, k = g[5], g[10]
        remote(gath.at[core], gath.at[core], k + 8, partner).wait()

    tok_send[...] = pack_tile(wide(tokens_ref[...]).reshape(AREA, WINDOWS, CHANNELS))
    cot_send[...] = pack_tile(wide(cot_ref[...]).reshape(AREA, WINDOWS, CHANNELS))
    pl.semaphore_wait(barrier, AREA)
    exchange_start(tok_send, tok_recv, 0)
    exchange_start(cot_send, cot_recv, 1)

    head_mask = low(wide(
        lax.broadcasted_iota(jnp.int32, (4 * AREA, LANES), 0) // AREA
        == lax.broadcasted_iota(jnp.int32, (4 * AREA, LANES), 1) // HEAD_DIM
    ))
    head_mask_two = jnp.concatenate([head_mask, head_mask], axis=1)
    head_wide = wide(head_mask_two)
    first_rows = lax.broadcasted_iota(jnp.int32, (LANES, LANES), 0) < AREA
    top = low(wide(first_rows))
    bottom = low(1.0 - wide(first_rows))
    for t in range(NUM_HEADS // 2):
        two = jnp.concatenate([bias_ref[2 * t], bias_ref[2 * t + 1]], axis=1)
        bias_t[t // 2, pl.ds((t % 2) * LANES, LANES), :] = jnp.concatenate([two, two], axis=0).T

    gain_one = gain_one_ref[...]
    gain_two = gain_two_ref[...]

    def to_rows(recv, dest):
        tile = wide(recv[...])
        for half in range(2):
            mix[half] = tile[:, 8 * half : 8 * half + 8, :].reshape(LOCAL, LANES)
        for w in range(WINDOWS):
            for half in range(2):
                dest[pl.ds(w * AREA, AREA), pl.ds(half * LANES, LANES)] = mix[half, pl.ds(w, AREA, stride=WINDOWS), :]

    def from_rows(values, send):
        for w in range(WINDOWS):
            for half in range(2):
                mix[half, pl.ds(w, AREA, stride=WINDOWS), :] = values[
                    w * AREA : (w + 1) * AREA, half * LANES : (half + 1) * LANES
                ]
        send[...] = low(jnp.concatenate(
            [mix[0].reshape(AREA, WINDOWS, LANES), mix[1].reshape(AREA, WINDOWS, LANES)], axis=1
        ))

    exchange_recv(tok_recv, 0)
    to_rows(tok_recv, x_ref)
    normed_one, inverse_one = norm_forward(x_ref[...])
    n1_ref[...] = normed_one
    n1_low[...] = low(normed_one * gain_one)
    qkv_ref[...] = low(dot_nn(n1_low[...], wqkv_ref[...]))

    def block(ref, b, part, half):
        return ref[pl.ds(b * LANES, LANES), pl.ds(part * CHANNELS + half * LANES, LANES)]

    def spread(tile):
        return jnp.concatenate([jnp.concatenate([tile[:AREA]] * 4, axis=0) * head_mask,
                                jnp.concatenate([tile[AREA:]] * 4, axis=0) * head_mask], axis=1)

    def diagonal(tile):
        return jnp.concatenate([tile * top, tile * bottom], axis=1)

    def own_window(tile):
        return jnp.where(first_rows, tile[:, :LANES], tile[:, LANES:])

    def own_heads(tile):
        folded = jnp.sum((tile * head_wide).reshape(4, AREA, 2 * LANES), axis=0)
        return jnp.concatenate([folded[:, :LANES], folded[:, LANES:]], axis=0)

    order = [(b, half) for b in range(PAIRS) for half in range(2)]
    for b, half in order:
        slot = 2 * b + half
        kbig_ref[slot] = spread(block(qkv_ref, b, 1, half))
        vbig_ref[slot] = spread(block(qkv_ref, b, 2, half))
        scores = dot_nt(kbig_ref[slot], diagonal(block(qkv_ref, b, 0, half))) * SCORE_SCALE + bias_t[half]
        scores = scores.reshape(4, AREA, LANES)
        raised = jnp.exp(scores - jnp.max(scores, axis=1, keepdims=True))
        probs = raised * (1.0 / jnp.sum(raised, axis=1, keepdims=True))
        probs = probs.reshape(4 * AREA, LANES)
        probs_ref[slot] = probs
        mixed = dot_tn(low(probs), vbig_ref[slot])
        att_ref[pl.ds(b * LANES, LANES), pl.ds(half * LANES, LANES)] = low(own_window(mixed))
    branch = low(dot_nn(att_ref[...], wproj_ref[...]))
    mid_ref[...] = wide(low(x_ref[...] + wide(branch)))

    normed_two, inverse_two = norm_forward(mid_ref[...])
    n2_ref[...] = normed_two
    n2_low[...] = low(normed_two * gain_two)
    exchange_recv(cot_recv, 1)
    to_rows(cot_recv, cot_w)
    cot_low[...] = low(cot_w[...])
    n2_turned = low((normed_two * gain_two)).T
    for j in range(4):
        cut = pl.ds(j * 256, 256)
        preact = dot_nn(n2_low[...], fc1_ref[:, cut])
        activation, slope = gelu_parts(preact)
        activation = low(activation)
        grad_pre = low(dot_nt(cot_low[...], fc2_ref[cut, :]) * slope)
        out_term = dot_nn(activation, fc2_ref[cut, :])
        grad_term = dot_nt(grad_pre, fc1_ref[:, cut])
        if j == 0:
            acc_ref[...] = out_term
            gnm_ref[...] = grad_term
        else:
            acc_ref[...] += out_term
            gnm_ref[...] += grad_term
        block_b = low(dot_tn(activation, cot_low[...]))
        block_a = low(dot_nn(n2_turned, grad_pre))
        for r in range(4):
            for c in range(2):
                part_b[j // 2, ((j % 2) * 4 + r) * 2 + c] = block_b[r * 64 : r * 64 + 64, c * LANES : (c + 1) * LANES]
                part_a[r // 2, (r % 2) * 8 + 2 * j + c] = block_a[r * 64 : r * 64 + 64, c * LANES : (c + 1) * LANES]
    core_start(parts[0])
    core_start(parts[1])
    from_rows(wide(low(mid_ref[...] + acc_ref[...])), out_send)
    exchange_start(out_send, out_back, 2)

    gnm = gnm_ref[...]
    normed_two = n2_ref[...]
    gain_row_two = jnp.sum(gnm * normed_two, axis=0, keepdims=True)
    gm_low[...] = low(cot_w[...] + norm_backward(gnm, normed_two, inverse_two, gain_two))
    gatt_ref[...] = low(dot_nt(gm_low[...], wproj_ref[...]))

    def put(ref, b, part, half, tile):
        ref[pl.ds(b * LANES, LANES), pl.ds(part * CHANNELS + half * LANES, LANES)] = low(tile)

    for n, (b, half) in enumerate(order):
        slot = 2 * b + half
        probs = probs_ref[slot]
        grad_diag = diagonal(block(gatt_ref, b, 0, half))
        grad_probs = dot_nt(vbig_ref[slot], grad_diag)
        put(gp_ref, b, 2, half, own_heads(dot_nn(low(probs), grad_diag)))
        weighted = (probs * grad_probs).reshape(4, AREA, LANES)
        total = jnp.sum(weighted, axis=1, keepdims=True)
        grad_scores = probs * (grad_probs.reshape(4, AREA, LANES) - total).reshape(4 * AREA, LANES)
        if b == 0:
            gbias[half] = grad_scores
        else:
            gbias[half] += grad_scores
        scores_low = low(grad_scores)
        put(gp_ref, b, 0, half, own_window(dot_tn(scores_low, kbig_ref[slot])) * SCORE_SCALE)
        query_diag = diagonal(block(qkv_ref, b, 0, half))
        put(gp_ref, b, 1, half, own_heads(dot_nn(scores_low, query_diag)) * SCORE_SCALE)
        if n == 2:
            plane_start(parts[0])
        if n == 4:
            plane_start(parts[1])

    grad_qkv = low(dot_tn(n1_low[...], gp_ref[...]))
    for h in range(2):
        for r in range(2):
            for c in range(6):
                part_c[h, r * 6 + c, pl.ds(0, 64), :] = grad_qkv[
                    h * 128 + r * 64 : h * 128 + r * 64 + 64, c * LANES : (c + 1) * LANES
                ]
    grad_proj = low(dot_tn(att_ref[...], gm_low[...]))
    for h in range(2):
        for r in range(2):
            for c in range(2):
                part_c[h, 12 + r * 2 + c, pl.ds(0, 64), :] = grad_proj[
                    h * 128 + r * 64 : h * 128 + r * 64 + 64, c * LANES : (c + 1) * LANES
                ]
    grad_normed_in = wide(low(dot_nt(gp_ref[...], wqkv_ref[...])))
    normed_one = n1_ref[...]
    gain_row_one = jnp.sum(grad_normed_in * normed_one, axis=0, keepdims=True)
    gains = jnp.concatenate(
        [gain_row_one[:, :LANES], gain_row_one[:, LANES:], gain_row_two[:, :LANES], gain_row_two[:, LANES:],
         jnp.zeros((4, LANES), F32)], axis=0,
    )
    for h in range(2):
        for t in range(2):
            tile = gbias[h, pl.ds(t * LANES, LANES), :]
            tile = (tile + pltpu.roll(tile, AREA, 1)).T
            for r in range(8):
                part_c[h, t * 8 + r, pl.ds(64, 16), :] = low(
                    jnp.concatenate([tile[8 * r : 8 * r + 8], gains], axis=0)
                )
    core_start(parts[2])
    grad_tokens = wide(gm_low[...]) + norm_backward(grad_normed_in, normed_one, inverse_one, gain_one)
    from_rows(wide(low(grad_tokens)), grad_send)
    exchange_start(grad_send, grad_back, 3)

    plane_start(parts[2])
    axis_start(parts[0])
    axis_start(parts[1])
    axis_start(parts[2])
    gather_start(parts[0])
    gather_start(parts[1])
    gather_start(parts[2])
    share_start(parts[0])
    share_start(parts[1])
    share_start(parts[2])
    exchange_recv(out_back, 2)
    exchange_recv(grad_back, 3)
    exchange_sent(tok_send, 0)
    exchange_sent(cot_send, 1)
    exchange_sent(out_send, 2)
    exchange_sent(grad_send, 3)
    for g in parts:
        share_wait(g)


def final_kernel(
    scale, out_back, grad_back, gath_a, gath_b, gath_c,
    out_ref, gtok_ref, gqkv_ref, gproj_ref, gbias_ref, gfc1_ref, gfc2_ref, gone_ref, gtwo_ref,
):
    for src, dst in ((out_back, out_ref), (grad_back, gtok_ref)):
        tile = wide(src[...])
        joined = jnp.concatenate([tile[:, :8, :], tile[:, 8:, :]], axis=2)
        dst[...] = low(joined.reshape(dst.shape))
    for h in range(2):
        for j in range(PIECES):
            gfc1_ref[pl.ds(h * 128 + (j // 8) * 64, 64), pl.ds((j % 8) * LANES, LANES)] = wide(gath_a[h, j]) * scale
            gfc2_ref[pl.ds(h * 512 + (j // 2) * 64, 64), pl.ds((j % 2) * LANES, LANES)] = wide(gath_b[h, j]) * scale
            tile = wide(gath_c[h, j, pl.ds(0, 64), :]) * scale
            if j < 12:
                gqkv_ref[pl.ds(h * 128 + (j // 6) * 64, 64), pl.ds((j % 6) * LANES, LANES)] = tile
            else:
                t = j - 12
                gproj_ref[pl.ds(h * 128 + (t // 2) * 64, 64), pl.ds((t % 2) * LANES, LANES)] = tile
            extra = wide(gath_c[h, j, pl.ds(64, 16), :])
            bias = extra[:8] * (scale * AREA)
            t, r = j // 8, j % 8
            gbias_ref[4 * h + 2 * t, pl.ds(8 * r, 8), :] = bias[:, :AREA]
            gbias_ref[4 * h + 2 * t + 1, pl.ds(8 * r, 8), :] = bias[:, AREA:]
            if h == 0 and j == 0:
                gone_ref[:, :LANES] = extra[8:9] * scale
                gone_ref[:, LANES:] = extra[9:10] * scale
                gtwo_ref[:, :LANES] = extra[10:11] * scale
                gtwo_ref[:, LANES:] = extra[11:12] * scale


VMEM = pl.BlockSpec(memory_space=pltpu.VMEM)


def body(tokens, cotangent, gain_one, qkv_weight, proj_weight, rel_bias, gain_two, fc_one, fc_two):
    tile_rows, tile_cols, channels = tokens.shape
    total_tokens = tile_rows * tile_cols * lax.axis_size("row") * lax.axis_size("col")
    grad_scale = total_tokens ** (-0.5)

    def shape(*dims, dtype=BF16):
        return jax.ShapeDtypeStruct(dims, dtype)

    def vmem(*dims, dtype=BF16):
        return pltpu.VMEM(dims, dtype)

    swap = (AREA, 16, LANES)
    ab, c = (PIECES, 64, LANES), (PIECES, 80, LANES)
    three = (ab, ab, c)
    swapped = pl.pallas_call(
        fused_kernel,
        out_shape=(shape(*swap), shape(*swap), shape(2, *ab), shape(2, *ab), shape(2, *c)),
        in_specs=[VMEM] * 9,
        out_specs=(VMEM,) * 5,
        scratch_shapes=[
            *[vmem(*swap) for _ in range(6)],
            *[vmem(2, *s) for s in three],
            *[vmem(*s) for s in three],
            *[vmem(*s) for s in three],
            *[vmem(*s) for s in three],
            *[vmem(4, *s[1:]) for s in three],
            vmem(2, LOCAL, LANES, dtype=F32),
            vmem(LOCAL, CHANNELS, dtype=F32),
            vmem(LOCAL, CHANNELS, dtype=F32),
            vmem(LOCAL, CHANNELS),
            vmem(LOCAL, CHANNELS, dtype=F32),
            vmem(LOCAL, CHANNELS),
            vmem(LOCAL, 3 * CHANNELS),
            vmem(LOCAL, CHANNELS),
            vmem(LOCAL, CHANNELS, dtype=F32),
            vmem(LOCAL, CHANNELS),
            vmem(LOCAL, CHANNELS, dtype=F32),
            vmem(LOCAL, CHANNELS, dtype=F32),
            vmem(LOCAL, CHANNELS, dtype=F32),
            vmem(LOCAL, CHANNELS),
            vmem(LOCAL, CHANNELS),
            vmem(LOCAL, 3 * CHANNELS),
            vmem(2, 4 * AREA, LANES, dtype=F32),
            vmem(2, 4 * AREA, LANES, dtype=F32),
            vmem(8, 4 * AREA, LANES, dtype=F32),
            vmem(8, 4 * AREA, 2 * LANES),
            vmem(8, 4 * AREA, 2 * LANES),
            pltpu.SemaphoreType.DMA((38,)),
        ],
        compiler_params=pltpu.CompilerParams(
            collective_id=0, has_side_effects=True, vmem_limit_bytes=48 * 1024 * 1024
        ),
        name="fused",
    )(
        tokens, cotangent, gain_one.reshape(1, -1), qkv_weight, proj_weight, rel_bias,
        gain_two.reshape(1, -1), fc_one, fc_two,
    )
    results = pl.pallas_call(
        functools.partial(final_kernel, grad_scale),
        out_shape=(
            shape(*tokens.shape), shape(*tokens.shape), shape(CHANNELS, 3 * CHANNELS, dtype=F32),
            shape(CHANNELS, CHANNELS, dtype=F32), shape(NUM_HEADS, AREA, AREA, dtype=F32),
            shape(CHANNELS, MLP_DIM, dtype=F32), shape(MLP_DIM, CHANNELS, dtype=F32),
            shape(1, CHANNELS, dtype=F32), shape(1, CHANNELS, dtype=F32),
        ),
        in_specs=[VMEM] * 5,
        out_specs=(VMEM,) * 9,
        compiler_params=pltpu.CompilerParams(vmem_limit_bytes=32 * 1024 * 1024),
        name="finish",
    )(*swapped)
    return (*results[:7], results[7].reshape(-1), results[8].reshape(-1))


def solution(mesh):
    in_specs = (P("row", "col", None), P("row", "col", None), P(), P(), P(), P(), P(), P(), P())
    out_specs = (P("row", "col", None), P("row", "col", None), P(), P(), P(), P(), P(), P(), P())
    return jax.shard_map(body, mesh=mesh, in_specs=in_specs, out_specs=out_specs, check_vma=False)
```

```python
import functools

import jax
import jax.numpy as jnp
from jax import lax
from jax.experimental import pallas as pl
from jax.experimental.pallas import tpu as pltpu
from jax.sharding import PartitionSpec as P

NUM_HEADS = 8
HEAD_DIM = 32
GRID_SIDE = 8
AREA = GRID_SIDE * GRID_SIDE
CHANNELS = 256
MLP_DIM = 1024
WINDOWS = 8
LOCAL = WINDOWS * AREA
PAIRS = 4
LANES = 128
PIECES = 16

EPSILON = 1e-05
ROOT_HALF = 0.7071067811865476
DENSITY = 0.3989422804014327
SCORE_SCALE = HEAD_DIM ** (-0.5)

MESH = pl.DeviceIdType.MESH
BF16 = jnp.bfloat16
F32 = jnp.float32


def low(values):
    return values.astype(BF16)


def wide(values):
    return values.astype(F32)


def dot_nn(a, b):
    return lax.dot_general(a, b, (((1,), (0,)), ((), ())), preferred_element_type=F32)


def dot_nt(a, b):
    return lax.dot_general(a, b, (((1,), (1,)), ((), ())), preferred_element_type=F32)


def dot_tn(a, b):
    return lax.dot_general(a, b, (((0,), (0,)), ((), ())), preferred_element_type=F32)


def norm_forward(values):
    centre = jnp.mean(values, axis=-1, keepdims=True)
    shifted = values - centre
    spread = jnp.mean(shifted * shifted, axis=-1, keepdims=True)
    inverse = lax.rsqrt(spread + EPSILON)
    return (shifted * inverse, inverse)


def norm_backward(upstream, normed, inverse, gain_vec):
    scaled = upstream * gain_vec
    mean_first = jnp.mean(scaled, axis=-1, keepdims=True)
    second = jnp.mean(scaled * normed, axis=-1, keepdims=True)
    return inverse * (scaled - mean_first - normed * second)


def gelu_parts(preact):
    normal_cdf = 0.5 * (1.0 + lax.erf(preact * ROOT_HALF))
    return (preact * normal_cdf, normal_cdf + preact * DENSITY * jnp.exp(-0.5 * preact * preact))


def device_at(x, y, z, core):
    return (y * 2 + x // 2, (z * 2 + x % 2) * 2 + core)


def pack_tile(tile):
    return low(jnp.concatenate([tile[:, :, :LANES], tile[:, :, LANES:]], axis=1))


def fused_kernel(
    tokens_in, cot_in, gain_one_in, wqkv_in, wproj_in, bias_in, gain_two_in, fc1_in, fc2_in,
    out_back, grad_back, gath_a, gath_b, gath_c,
    tok_send, cot_send, out_send, grad_send, tok_recv, cot_recv,
    part_a, part_b, part_c, crecv_a, crecv_b, crecv_c, psend_a, psend_b, psend_c,
    precv_a, precv_b, precv_c, axis_a, axis_b, axis_c, total_a, total_b, total_c,
    mix, x_ref, cot_w, cot_low, n1_ref, n1_low, qkv_ref, att_ref, n2_ref, n2_low, mid_ref,
    acc_ref, gnm_ref, gm_low, gatt_ref, gp_ref, bias_t, gbias, probs_ref, kbig_ref, vbig_ref,
    tokens_ref, cot_ref, gain_one_ref, wqkv_ref, wproj_ref, bias_ref, gain_two_ref, fc1_ref, fc2_ref,
    sems, load_sems,
):
    row, col = lax.axis_index("row"), lax.axis_index("col")
    core = col % 2
    me = row * GRID_SIDE + col // 2
    x, y, z = (row % 2) * 2 + (col // 2) % 2, row // 2, col // 4
    partner = (row, col + 1 - 2 * core)

    def chip(p):
        return (p // GRID_SIDE, (p % GRID_SIDE) * 2 + core)

    loads = [
        pltpu.make_async_copy(src, dst, load_sems.at[n])
        for n, (src, dst) in enumerate((
            (tokens_in, tokens_ref), (cot_in, cot_ref), (gain_one_in, gain_one_ref), (wqkv_in, wqkv_ref),
            (bias_in, bias_ref), (wproj_in, wproj_ref), (gain_two_in, gain_two_ref), (fc1_in, fc1_ref),
            (fc2_in, fc2_ref),
        ))
    ]
    for load in loads:
        load.start()

    barrier = pltpu.get_barrier_semaphore()

    def greet(i, carry):
        pl.semaphore_signal(barrier, inc=1, device_id=chip(lax.rem(me + i, AREA)), device_id_type=MESH)
        return carry

    lax.fori_loop(1, AREA, greet, 0)
    pl.semaphore_signal(barrier, inc=1, device_id=partner, device_id_type=MESH)

    def exchange_start(send, recv, k):
        def step(i, carry):
            p = lax.rem(me + i, AREA)
            pltpu.make_async_remote_copy(
                src_ref=send.at[p], dst_ref=recv.at[me], send_sem=sems.at[2 * k], recv_sem=sems.at[2 * k + 1],
                device_id=chip(p), device_id_type=MESH,
            ).start()
            return carry

        lax.fori_loop(1, AREA, step, 0)
        if k < 2:
            recv[me] = send[me]
        else:
            own_copy(send, recv, k).start()

    def own_copy(send, recv, k):
        return pltpu.make_async_copy(send.at[me], recv.at[me], sems.at[42 + k])

    def drain(ref, sem):
        pltpu.make_async_copy(ref, ref, sem).wait()

    def exchange_recv(recv, k):
        drain(recv.at[pl.ds(0, AREA - 1)], sems.at[2 * k + 1])

    def exchange_sent(send, k):
        drain(send.at[pl.ds(0, AREA - 1)], sems.at[2 * k])

    def device_a(j):
        return device_at(x, j // 4, j % 4, core)

    def device_b(j):
        return device_at(j % 4, y, j // 4, core)

    def device_c(j):
        return device_at(j % 4, j // 4, z, core)

    parts = (
        (part_a, crecv_a, psend_a, precv_a, axis_a, total_a, gath_a, device_a, y * 4 + z,
         lambda t: device_at(t, y, z, core), x, 8),
        (part_b, crecv_b, psend_b, precv_b, axis_b, total_b, gath_b, device_b, z * 4 + x,
         lambda t: device_at(x, t, z, core), y, 20),
        (part_c, crecv_c, psend_c, precv_c, axis_c, total_c, gath_c, device_c, y * 4 + x,
         lambda t: device_at(x, y, t, core), z, 32),
    )

    def remote(src, dst, k, device):
        return pltpu.make_async_remote_copy(
            src_ref=src, dst_ref=dst, send_sem=sems.at[k], recv_sem=sems.at[k + 1],
            device_id=device, device_id_type=MESH,
        )

    def core_start(g):
        part, crecv, _, _, _, _, _, _, _, _, _, k = g
        remote(part.at[1 - core], crecv, k, partner).start()

    def plane_start(g):
        part, crecv, psend, precv, _, _, _, where, mine, _, _, k = g
        drain(crecv, sems.at[k + 1])
        psend[...] = low(wide(part[core]) + wide(crecv[...]))

        def step(i, carry):
            j = lax.rem(mine + i, PIECES)
            remote(psend.at[j], precv.at[mine], k + 2, where(j)).start()
            return carry

        lax.fori_loop(1, PIECES, step, 0)
        precv[mine] = psend[mine]

    def axis_start(g):
        _, _, _, precv, axis, _, _, _, _, along, place, k = g
        drain(precv.at[pl.ds(0, PIECES - 1)], sems.at[k + 3])
        axis[place] = low(jnp.sum(wide(precv[...]), axis=0))
        for i in range(1, 4):
            remote(axis.at[place], axis.at[place], k + 4, along(lax.rem(place + i, 4))).start()

    def total_copy(g):
        _, _, _, _, _, total, gath, _, mine, _, _, k = g
        return pltpu.make_async_copy(total, gath.at[core, mine], sems.at[k + 10])

    def gather_start(g):
        _, _, _, _, axis, total, gath, where, mine, _, _, k = g
        drain(axis.at[pl.ds(0, 3)], sems.at[k + 5])
        total[...] = low(jnp.sum(wide(axis[...]), axis=0))

        def step(i, carry):
            j = lax.rem(mine + i, PIECES)
            remote(total, gath.at[core, mine], k + 6, where(j)).start()
            return carry

        lax.fori_loop(1, PIECES, step, 0)
        total_copy(g).start()

    def share_start(g):
        _, _, _, _, _, _, gath, _, _, _, _, k = g
        drain(gath.at[core, pl.ds(0, PIECES - 1)], sems.at[k + 7])
        total_copy(g).wait()
        remote(gath.at[core], gath.at[core], k + 8, partner).start()

    def share_wait(g):
        part, crecv, psend, precv, axis, total, gath, _, _, _, _, k = g
        drain(gath.at[core], sems.at[k + 9])
        drain(crecv, sems.at[k])
        drain(psend.at[pl.ds(0, PIECES - 1)], sems.at[k + 2])
        drain(axis.at[pl.ds(0, 3)], sems.at[k + 4])
        drain(psend.at[pl.ds(0, PIECES - 1)], sems.at[k + 6])
        drain(crecv, sems.at[k + 8])

    loads[0].wait()
    tok_send[...] = pack_tile(wide(tokens_ref[...]).reshape(AREA, WINDOWS, CHANNELS))
    pl.semaphore_wait(barrier, AREA)
    exchange_start(tok_send, tok_recv, 0)
    loads[1].wait()
    cot_send[...] = pack_tile(wide(cot_ref[...]).reshape(AREA, WINDOWS, CHANNELS))
    exchange_start(cot_send, cot_recv, 1)
    for load in loads[2:]:
        load.wait()

    head_mask = low(wide(
        lax.broadcasted_iota(jnp.int32, (4 * AREA, LANES), 0) // AREA
        == lax.broadcasted_iota(jnp.int32, (4 * AREA, LANES), 1) // HEAD_DIM
    ))
    head_mask_two = jnp.concatenate([head_mask, head_mask], axis=1)
    head_wide = wide(head_mask_two)
    first_rows = lax.broadcasted_iota(jnp.int32, (LANES, LANES), 0) < AREA
    top = low(wide(first_rows))
    bottom = low(1.0 - wide(first_rows))
    for t in range(NUM_HEADS // 2):
        two = jnp.concatenate([bias_ref[2 * t], bias_ref[2 * t + 1]], axis=1)
        bias_t[t // 2, pl.ds((t % 2) * LANES, LANES), :] = jnp.concatenate([two, two], axis=0).T

    gain_one = gain_one_ref[...]
    gain_two = gain_two_ref[...]

    def to_rows(recv, dest):
        tile = wide(recv[...])
        for half in range(2):
            mix[half] = tile[:, 8 * half : 8 * half + 8, :].reshape(LOCAL, LANES)
        for w in range(WINDOWS):
            for half in range(2):
                dest[pl.ds(w * AREA, AREA), pl.ds(half * LANES, LANES)] = mix[half, pl.ds(w, AREA, stride=WINDOWS), :]

    def from_rows(values, send):
        for w in range(WINDOWS):
            for half in range(2):
                mix[half, pl.ds(w, AREA, stride=WINDOWS), :] = values[
                    w * AREA : (w + 1) * AREA, half * LANES : (half + 1) * LANES
                ]
        send[...] = low(jnp.concatenate(
            [mix[0].reshape(AREA, WINDOWS, LANES), mix[1].reshape(AREA, WINDOWS, LANES)], axis=1
        ))

    exchange_recv(tok_recv, 0)
    to_rows(tok_recv, x_ref)
    normed_one, inverse_one = norm_forward(x_ref[...])
    n1_ref[...] = normed_one
    n1_low[...] = low(normed_one * gain_one)
    qkv_ref[...] = low(dot_nn(n1_low[...], wqkv_ref[...]))

    def block(ref, b, part, half):
        return ref[pl.ds(b * LANES, LANES), pl.ds(part * CHANNELS + half * LANES, LANES)]

    def spread(tile):
        return jnp.concatenate([jnp.concatenate([tile[:AREA]] * 4, axis=0) * head_mask,
                                jnp.concatenate([tile[AREA:]] * 4, axis=0) * head_mask], axis=1)

    def diagonal(tile):
        return jnp.concatenate([tile * top, tile * bottom], axis=1)

    def own_window(tile):
        return jnp.where(first_rows, tile[:, :LANES], tile[:, LANES:])

    def own_heads(tile):
        folded = jnp.sum((tile * head_wide).reshape(4, AREA, 2 * LANES), axis=0)
        return jnp.concatenate([folded[:, :LANES], folded[:, LANES:]], axis=0)

    order = [(b, half) for b in range(PAIRS) for half in range(2)]
    for b, half in order:
        slot = 2 * b + half
        kbig_ref[slot] = spread(block(qkv_ref, b, 1, half))
        vbig_ref[slot] = spread(block(qkv_ref, b, 2, half))
        scores = dot_nt(kbig_ref[slot], diagonal(block(qkv_ref, b, 0, half))) * SCORE_SCALE + bias_t[half]
        scores = scores.reshape(4, AREA, LANES)
        raised = jnp.exp(scores - jnp.max(scores, axis=1, keepdims=True))
        probs = raised * (1.0 / jnp.sum(raised, axis=1, keepdims=True))
        probs = probs.reshape(4 * AREA, LANES)
        probs_ref[slot] = probs
        mixed = dot_tn(low(probs), vbig_ref[slot])
        att_ref[pl.ds(b * LANES, LANES), pl.ds(half * LANES, LANES)] = low(own_window(mixed))
    branch = low(dot_nn(att_ref[...], wproj_ref[...]))
    mid_ref[...] = wide(low(x_ref[...] + wide(branch)))

    normed_two, inverse_two = norm_forward(mid_ref[...])
    n2_ref[...] = normed_two
    n2_low[...] = low(normed_two * gain_two)
    exchange_recv(cot_recv, 1)
    to_rows(cot_recv, cot_w)
    cot_low[...] = low(cot_w[...])
    n2_turned = low((normed_two * gain_two)).T
    for j in range(4):
        cut = pl.ds(j * 256, 256)
        preact = dot_nn(n2_low[...], fc1_ref[:, cut])
        activation, slope = gelu_parts(preact)
        activation = low(activation)
        grad_pre = low(dot_nt(cot_low[...], fc2_ref[cut, :]) * slope)
        out_term = dot_nn(activation, fc2_ref[cut, :])
        grad_term = dot_nt(grad_pre, fc1_ref[:, cut])
        if j == 0:
            acc_ref[...] = out_term
            gnm_ref[...] = grad_term
        else:
            acc_ref[...] += out_term
            gnm_ref[...] += grad_term
        block_b = low(dot_tn(activation, cot_low[...]))
        block_a = low(dot_nn(n2_turned, grad_pre))
        for r in range(4):
            for c in range(2):
                part_b[j // 2, ((j % 2) * 4 + r) * 2 + c, pl.ds(0, 64), :] = block_b[r * 64 : r * 64 + 64, c * LANES : (c + 1) * LANES]
                part_a[r // 2, (r % 2) * 8 + 2 * j + c] = block_a[r * 64 : r * 64 + 64, c * LANES : (c + 1) * LANES]
    core_start(parts[0])
    from_rows(wide(low(mid_ref[...] + acc_ref[...])), out_send)
    exchange_start(out_send, out_back, 2)

    gnm = gnm_ref[...]
    normed_two = n2_ref[...]
    gain_row_two = jnp.sum(gnm * normed_two, axis=0, keepdims=True)
    gm_low[...] = low(cot_w[...] + norm_backward(gnm, normed_two, inverse_two, gain_two))
    grad_proj = low(dot_tn(att_ref[...], gm_low[...]))
    for h in range(2):
        for r in range(8):
            for c in range(2):
                part_b[h, r * 2 + c, pl.ds(64, 16), :] = grad_proj[
                    h * 128 + r * 16 : h * 128 + r * 16 + 16, c * LANES : (c + 1) * LANES
                ]
    core_start(parts[1])
    gatt_ref[...] = low(dot_nt(gm_low[...], wproj_ref[...]))

    def put(ref, b, part, half, tile):
        ref[pl.ds(b * LANES, LANES), pl.ds(part * CHANNELS + half * LANES, LANES)] = low(tile)

    for n, (b, half) in enumerate(order):
        slot = 2 * b + half
        probs = probs_ref[slot]
        grad_diag = diagonal(block(gatt_ref, b, 0, half))
        grad_probs = dot_nt(vbig_ref[slot], grad_diag)
        put(gp_ref, b, 2, half, own_heads(dot_nn(low(probs), grad_diag)))
        weighted = (probs * grad_probs).reshape(4, AREA, LANES)
        total = jnp.sum(weighted, axis=1, keepdims=True)
        grad_scores = probs * (grad_probs.reshape(4, AREA, LANES) - total).reshape(4 * AREA, LANES)
        if b == 0:
            gbias[half] = grad_scores
        else:
            gbias[half] += grad_scores
        scores_low = low(grad_scores)
        put(gp_ref, b, 0, half, own_window(dot_tn(scores_low, kbig_ref[slot])) * SCORE_SCALE)
        query_diag = diagonal(block(qkv_ref, b, 0, half))
        put(gp_ref, b, 1, half, own_heads(dot_nn(scores_low, query_diag)) * SCORE_SCALE)
        if n == 2:
            plane_start(parts[0])
        if n == 4:
            plane_start(parts[1])

    grad_qkv = low(dot_tn(n1_low[...], gp_ref[...]))
    for h in range(2):
        for r in range(8):
            for c in range(6):
                part_c[h, r * 2 + c // 3, pl.ds((c % 3) * 16, 16), :] = grad_qkv[
                    h * 128 + r * 16 : h * 128 + r * 16 + 16, c * LANES : (c + 1) * LANES
                ]
    grad_normed_in = wide(low(dot_nt(gp_ref[...], wqkv_ref[...])))
    normed_one = n1_ref[...]
    gain_row_one = jnp.sum(grad_normed_in * normed_one, axis=0, keepdims=True)
    gains = jnp.concatenate(
        [gain_row_one[:, :LANES], gain_row_one[:, LANES:], gain_row_two[:, :LANES], gain_row_two[:, LANES:],
         jnp.zeros((4, LANES), F32)], axis=0,
    )
    for h in range(2):
        for t in range(2):
            tile = gbias[h, pl.ds(t * LANES, LANES), :]
            tile = (tile + pltpu.roll(tile, AREA, 1)).T
            for r in range(8):
                part_c[h, t * 8 + r, pl.ds(48, 16), :] = low(
                    jnp.concatenate([tile[8 * r : 8 * r + 8], gains], axis=0)
                )
    core_start(parts[2])
    grad_tokens = wide(gm_low[...]) + norm_backward(grad_normed_in, normed_one, inverse_one, gain_one)
    from_rows(wide(low(grad_tokens)), grad_send)

    plane_start(parts[2])
    exchange_start(grad_send, grad_back, 3)
    axis_start(parts[0])
    axis_start(parts[1])
    axis_start(parts[2])
    gather_start(parts[0])
    gather_start(parts[1])
    gather_start(parts[2])
    share_start(parts[0])
    share_start(parts[1])
    share_start(parts[2])
    exchange_recv(out_back, 2)
    exchange_recv(grad_back, 3)
    own_copy(out_send, out_back, 2).wait()
    own_copy(grad_send, grad_back, 3).wait()
    for k, send in enumerate((tok_send, cot_send, out_send, grad_send)):
        exchange_sent(send, k)
    for g in parts:
        share_wait(g)


def final_kernel(
    scale, out_back, grad_back, gath_a, gath_b, gath_c,
    out_ref, gtok_ref, gqkv_ref, gproj_ref, gbias_ref, gfc1_ref, gfc2_ref, gone_ref, gtwo_ref,
    *scratch,
):
    sources, (out_v, gtok_v, gqkv_v, gproj_v, gbias_v, gfc1_v, gfc2_v, gone_v, gtwo_v) = scratch[:5], scratch[5:14]
    load_sems, save_sems = scratch[14:]
    loads = [
        pltpu.make_async_copy(src, dst, load_sems.at[n])
        for n, (src, dst) in enumerate(zip((out_back, grad_back, gath_a, gath_b, gath_c), sources))
    ]
    for load in loads:
        load.start()
    saves = [
        pltpu.make_async_copy(src, dst, save_sems.at[n])
        for n, (src, dst) in enumerate((
            (out_v, out_ref), (gtok_v, gtok_ref), (gfc1_v, gfc1_ref), (gfc2_v, gfc2_ref), (gproj_v, gproj_ref),
            (gqkv_v, gqkv_ref), (gbias_v, gbias_ref), (gone_v, gone_ref), (gtwo_v, gtwo_ref),
        ))
    ]
    for n, dst in enumerate((out_v, gtok_v)):
        loads[n].wait()
        tile = wide(sources[n][...])
        joined = jnp.concatenate([tile[:, :8, :], tile[:, 8:, :]], axis=2)
        dst[...] = low(joined.reshape(dst.shape))
        saves[n].start()
    halves = [(h, j) for h in range(2) for j in range(PIECES)]
    loads[2].wait()
    for h, j in halves:
        gfc1_v[pl.ds(h * 128 + (j // 8) * 64, 64), pl.ds((j % 8) * LANES, LANES)] = wide(sources[2][h, j]) * scale
    saves[2].start()
    loads[3].wait()
    for h, j in halves:
        tile = wide(sources[3][h, j]) * scale
        gfc2_v[pl.ds(h * 512 + (j // 2) * 64, 64), pl.ds((j % 2) * LANES, LANES)] = tile[:64]
        gproj_v[pl.ds(h * 128 + (j // 2) * 16, 16), pl.ds((j % 2) * LANES, LANES)] = tile[64:]
    saves[3].start()
    saves[4].start()
    loads[4].wait()
    for h, j in halves:
        tile = wide(sources[4][h, j]) * scale
        for c in range(3):
            gqkv_v[pl.ds(h * 128 + (j // 2) * 16, 16), pl.ds(((j % 2) * 3 + c) * LANES, LANES)] = (
                tile[16 * c : 16 * c + 16]
            )
        bias = tile[48:56] * AREA
        t, r = j // 8, j % 8
        gbias_v[4 * h + 2 * t, pl.ds(8 * r, 8), :] = bias[:, :AREA]
        gbias_v[4 * h + 2 * t + 1, pl.ds(8 * r, 8), :] = bias[:, AREA:]
        if h == 0 and j == 0:
            gone_v[:, :LANES] = tile[56:57]
            gone_v[:, LANES:] = tile[57:58]
            gtwo_v[:, :LANES] = tile[58:59]
            gtwo_v[:, LANES:] = tile[59:60]
    for save in saves[5:]:
        save.start()
    for save in saves:
        save.wait()


HBM = pl.BlockSpec(memory_space=pltpu.HBM)


def body(tokens, cotangent, gain_one, qkv_weight, proj_weight, rel_bias, gain_two, fc_one, fc_two):
    tile_rows, tile_cols, channels = tokens.shape
    total_tokens = tile_rows * tile_cols * lax.axis_size("row") * lax.axis_size("col")
    grad_scale = total_tokens ** (-0.5)

    def shape(*dims, dtype=BF16):
        return jax.ShapeDtypeStruct(dims, dtype)

    def vmem(*dims, dtype=BF16):
        return pltpu.VMEM(dims, dtype)

    swap = (AREA, 16, LANES)
    three = ((PIECES, 64, LANES), (PIECES, 80, LANES), (PIECES, 64, LANES))
    swapped = pl.pallas_call(
        fused_kernel,
        out_shape=(shape(*swap), shape(*swap), *[shape(2, *s) for s in three]),
        in_specs=[HBM] * 9,
        out_specs=(HBM,) * 5,
        scratch_shapes=[
            *[vmem(*swap) for _ in range(6)],
            *[vmem(2, *s) for s in three],
            *[vmem(*s) for s in three],
            *[vmem(*s) for s in three],
            *[vmem(*s) for s in three],
            *[vmem(4, *s[1:]) for s in three],
            *[vmem(*s[1:]) for s in three],
            vmem(2, LOCAL, LANES, dtype=F32),
            vmem(LOCAL, CHANNELS, dtype=F32),
            vmem(LOCAL, CHANNELS, dtype=F32),
            vmem(LOCAL, CHANNELS),
            vmem(LOCAL, CHANNELS, dtype=F32),
            vmem(LOCAL, CHANNELS),
            vmem(LOCAL, 3 * CHANNELS),
            vmem(LOCAL, CHANNELS),
            vmem(LOCAL, CHANNELS, dtype=F32),
            vmem(LOCAL, CHANNELS),
            vmem(LOCAL, CHANNELS, dtype=F32),
            vmem(LOCAL, CHANNELS, dtype=F32),
            vmem(LOCAL, CHANNELS, dtype=F32),
            vmem(LOCAL, CHANNELS),
            vmem(LOCAL, CHANNELS),
            vmem(LOCAL, 3 * CHANNELS),
            vmem(2, 4 * AREA, LANES, dtype=F32),
            vmem(2, 4 * AREA, LANES, dtype=F32),
            vmem(8, 4 * AREA, LANES, dtype=F32),
            vmem(8, 4 * AREA, 2 * LANES),
            vmem(8, 4 * AREA, 2 * LANES),
            vmem(*tokens.shape),
            vmem(*cotangent.shape),
            vmem(1, CHANNELS, dtype=F32),
            vmem(*qkv_weight.shape),
            vmem(*proj_weight.shape),
            vmem(*rel_bias.shape, dtype=F32),
            vmem(1, CHANNELS, dtype=F32),
            vmem(*fc_one.shape),
            vmem(*fc_two.shape),
            pltpu.SemaphoreType.DMA((46,)),
            pltpu.SemaphoreType.DMA((9,)),
        ],
        compiler_params=pltpu.CompilerParams(
            collective_id=0, has_side_effects=True, vmem_limit_bytes=60 * 1024 * 1024
        ),
        name="fused",
    )(
        tokens, cotangent, gain_one.reshape(1, -1), qkv_weight, proj_weight, rel_bias,
        gain_two.reshape(1, -1), fc_one, fc_two,
    )
    outs = (
        tokens.shape, tokens.shape, qkv_weight.shape, proj_weight.shape, rel_bias.shape, fc_one.shape, fc_two.shape,
        (1, CHANNELS), (1, CHANNELS),
    )
    types = (BF16, BF16, *[F32] * 7)
    results = pl.pallas_call(
        functools.partial(final_kernel, grad_scale),
        out_shape=tuple(shape(*dims, dtype=t) for dims, t in zip(outs, types)),
        in_specs=[HBM] * 5,
        out_specs=(HBM,) * 9,
        scratch_shapes=[
            vmem(*swap), vmem(*swap), *[vmem(2, *s) for s in three],
            *[vmem(*dims, dtype=t) for dims, t in zip(outs, types)],
            pltpu.SemaphoreType.DMA((5,)),
            pltpu.SemaphoreType.DMA((9,)),
        ],
        compiler_params=pltpu.CompilerParams(vmem_limit_bytes=60 * 1024 * 1024),
        name="finish",
    )(*swapped)
    return (*results[:7], results[7].reshape(-1), results[8].reshape(-1))


def solution(mesh):
    in_specs = (P("row", "col", None), P("row", "col", None), P(), P(), P(), P(), P(), P(), P())
    out_specs = (P("row", "col", None), P("row", "col", None), P(), P(), P(), P(), P(), P(), P())
    return jax.shard_map(body, mesh=mesh, in_specs=in_specs, out_specs=out_specs, check_vma=False)
```

```python
import functools

import jax
import jax.numpy as jnp
from jax import lax
from jax.experimental import pallas as pl
from jax.experimental.pallas import tpu as pltpu
from jax.sharding import PartitionSpec as P

NUM_HEADS = 8
HEAD_DIM = 32
GRID_SIDE = 8
AREA = GRID_SIDE * GRID_SIDE
CHANNELS = 256
MLP_DIM = 1024
WINDOWS = 8
LOCAL = WINDOWS * AREA
PAIRS = 4
LANES = 128
PIECES = 16

EPSILON = 1e-05
ROOT_HALF = 0.7071067811865476
DENSITY = 0.3989422804014327
SCORE_SCALE = HEAD_DIM ** (-0.5)

MESH = pl.DeviceIdType.MESH
BF16 = jnp.bfloat16
F32 = jnp.float32


def low(values):
    return values.astype(BF16)


def wide(values):
    return values.astype(F32)


def dot_nn(a, b):
    return lax.dot_general(a, b, (((1,), (0,)), ((), ())), preferred_element_type=F32)


def dot_nt(a, b):
    return lax.dot_general(a, b, (((1,), (1,)), ((), ())), preferred_element_type=F32)


def dot_tn(a, b):
    return lax.dot_general(a, b, (((0,), (0,)), ((), ())), preferred_element_type=F32)


def norm_forward(values):
    centre = jnp.mean(values, axis=-1, keepdims=True)
    shifted = values - centre
    spread = jnp.mean(shifted * shifted, axis=-1, keepdims=True)
    inverse = lax.rsqrt(spread + EPSILON)
    return (shifted * inverse, inverse)


def norm_backward(upstream, normed, inverse, gain_vec):
    scaled = upstream * gain_vec
    mean_first = jnp.mean(scaled, axis=-1, keepdims=True)
    second = jnp.mean(scaled * normed, axis=-1, keepdims=True)
    return inverse * (scaled - mean_first - normed * second)


def gelu_parts(preact):
    normal_cdf = 0.5 * (1.0 + lax.erf(preact * ROOT_HALF))
    return (preact * normal_cdf, normal_cdf + preact * DENSITY * jnp.exp(-0.5 * preact * preact))


def hops(steps):
    return sum(min(d, 4 - d) for d in steps)


PLANE_STEPS = sorted(((a, b) for a in range(4) for b in range(4) if a or b), key=hops, reverse=True)
CHIP_STEPS = sorted(
    ((a, b, c) for a in range(4) for b in range(4) for c in range(4) if a or b or c), key=hops, reverse=True
)


def pack_tile(tile):
    return low(jnp.concatenate([tile[:, :, :LANES], tile[:, :, LANES:]], axis=1))


def fused_kernel(
    tokens_in, cot_in, gain_one_in, wqkv_in, wproj_in, bias_in, gain_two_in, fc1_in, fc2_in,
    out_back, grad_back, gath_a, gath_b, gath_c,
    tok_send, cot_send, out_send, grad_send, tok_recv, cot_recv,
    part_a, part_b, part_c, crecv_a, crecv_b, crecv_c, psend_a, psend_b, psend_c,
    precv_a, precv_b, precv_c, axis_a, axis_b, axis_c, total_a, total_b, total_c,
    mix, x_ref, cot_w, cot_low, n1_ref, n1_low, qkv_ref, att_ref, n2_ref, n2_low, mid_ref,
    acc_ref, gnm_ref, gm_low, gatt_ref, gp_ref, bias_t, gbias, probs_ref, kbig_ref, vbig_ref,
    tokens_ref, cot_ref, gain_one_ref, wqkv_ref, wproj_ref, bias_ref, gain_two_ref, fc1_ref, fc2_ref,
    sems, load_sems,
):
    row, col = lax.axis_index("row"), lax.axis_index("col")
    core = col % 2
    me = row * GRID_SIDE + col // 2
    x, y, z = (row % 2) * 2 + (col // 2) % 2, row // 2, col // 4
    partner = (row, col + 1 - 2 * core)

    xs, ys, zs = ([(v + d) % 4 for d in range(4)] for v in (x, y, z))
    col_x, row_x = [v % 2 for v in xs], [v // 2 for v in xs]

    def device(dx, dy, dz):
        return (ys[dy] * 2 + row_x[dx], (zs[dz] * 2 + col_x[dx]) * 2 + core)

    peers = []
    for steps in CHIP_STEPS:
        peer_row, peer_col = device(*steps)
        peers.append((peer_row * GRID_SIDE + peer_col // 2, (peer_row, peer_col)))

    loads = [
        pltpu.make_async_copy(src, dst, load_sems.at[n])
        for n, (src, dst) in enumerate((
            (tokens_in, tokens_ref), (cot_in, cot_ref), (gain_one_in, gain_one_ref), (wqkv_in, wqkv_ref),
            (bias_in, bias_ref), (wproj_in, wproj_ref), (gain_two_in, gain_two_ref), (fc1_in, fc1_ref),
            (fc2_in, fc2_ref),
        ))
    ]
    for load in loads:
        load.start()

    barrier = pltpu.get_barrier_semaphore()

    for _, peer in peers:
        pl.semaphore_signal(barrier, inc=1, device_id=peer, device_id_type=MESH)
    pl.semaphore_signal(barrier, inc=1, device_id=partner, device_id_type=MESH)

    def exchange_start(send, recv, k):
        for p, peer in peers:
            remote(send.at[p], recv.at[me], 2 * k, peer).start()
        if k < 2:
            recv[me] = send[me]
        else:
            own_copy(send, recv, k).start()

    def own_copy(send, recv, k):
        return pltpu.make_async_copy(send.at[me], recv.at[me], sems.at[42 + k])

    def drain(ref, sem):
        pltpu.make_async_copy(ref, ref, sem).wait()

    def exchange_recv(recv, k):
        drain(recv.at[pl.ds(0, AREA - 1)], sems.at[2 * k + 1])

    def exchange_sent(send, k):
        drain(send.at[pl.ds(0, AREA - 1)], sems.at[2 * k])

    def plane_a(a, b):
        return (ys[a] * 4 + zs[b], device(0, a, b))

    def plane_b(a, b):
        return (zs[a] * 4 + xs[b], device(b, 0, a))

    def plane_c(a, b):
        return (ys[a] * 4 + xs[b], device(b, a, 0))

    parts = (
        (part_a, crecv_a, psend_a, precv_a, axis_a, total_a, gath_a, plane_a, y * 4 + z,
         lambda d: device(d, 0, 0), x, 8),
        (part_b, crecv_b, psend_b, precv_b, axis_b, total_b, gath_b, plane_b, z * 4 + x,
         lambda d: device(0, d, 0), y, 20),
        (part_c, crecv_c, psend_c, precv_c, axis_c, total_c, gath_c, plane_c, y * 4 + x,
         lambda d: device(0, 0, d), z, 32),
    )

    def remote(src, dst, k, device):
        return pltpu.make_async_remote_copy(
            src_ref=src, dst_ref=dst, send_sem=sems.at[k], recv_sem=sems.at[k + 1],
            device_id=device, device_id_type=MESH,
        )

    def core_start(g):
        part, crecv, _, _, _, _, _, _, _, _, _, k = g
        remote(part.at[1 - core], crecv, k, partner).start()

    def plane_start(g):
        part, crecv, psend, precv, _, _, _, where, mine, _, _, k = g
        drain(crecv, sems.at[k + 1])
        psend[...] = low(wide(part[core]) + wide(crecv[...]))

        for steps in PLANE_STEPS:
            j, peer = where(*steps)
            remote(psend.at[j], precv.at[mine], k + 2, peer).start()
        precv[mine] = psend[mine]

    def axis_start(g):
        _, _, _, precv, axis, _, _, _, _, along, place, k = g
        drain(precv.at[pl.ds(0, PIECES - 1)], sems.at[k + 3])
        axis[place] = low(jnp.sum(wide(precv[...]), axis=0))
        for i in range(1, 4):
            remote(axis.at[place], axis.at[place], k + 4, along(i)).start()

    def total_copy(g):
        _, _, _, _, _, total, gath, _, mine, _, _, k = g
        return pltpu.make_async_copy(total, gath.at[core, mine], sems.at[k + 10])

    def gather_start(g):
        _, _, _, _, axis, total, gath, where, mine, _, _, k = g
        drain(axis.at[pl.ds(0, 3)], sems.at[k + 5])
        total[...] = low(jnp.sum(wide(axis[...]), axis=0))

        for steps in PLANE_STEPS:
            remote(total, gath.at[core, mine], k + 6, where(*steps)[1]).start()
        total_copy(g).start()

    def share_start(g):
        _, _, _, _, _, _, gath, _, _, _, _, k = g
        drain(gath.at[core, pl.ds(0, PIECES - 1)], sems.at[k + 7])
        total_copy(g).wait()
        remote(gath.at[core], gath.at[core], k + 8, partner).start()

    def share_wait(g):
        part, crecv, psend, precv, axis, total, gath, _, _, _, _, k = g
        drain(gath.at[core], sems.at[k + 9])
        drain(crecv, sems.at[k])
        drain(psend.at[pl.ds(0, PIECES - 1)], sems.at[k + 2])
        drain(axis.at[pl.ds(0, 3)], sems.at[k + 4])
        drain(psend.at[pl.ds(0, PIECES - 1)], sems.at[k + 6])
        drain(crecv, sems.at[k + 8])

    loads[0].wait()
    tok_send[...] = pack_tile(wide(tokens_ref[...]).reshape(AREA, WINDOWS, CHANNELS))
    pl.semaphore_wait(barrier, AREA)
    exchange_start(tok_send, tok_recv, 0)
    for load in loads[2:]:
        load.wait()

    head_mask = low(wide(
        lax.broadcasted_iota(jnp.int32, (4 * AREA, LANES), 0) // AREA
        == lax.broadcasted_iota(jnp.int32, (4 * AREA, LANES), 1) // HEAD_DIM
    ))
    head_mask_two = jnp.concatenate([head_mask, head_mask], axis=1)
    head_wide = wide(head_mask_two)
    first_rows = lax.broadcasted_iota(jnp.int32, (LANES, LANES), 0) < AREA
    top = low(wide(first_rows))
    bottom = low(1.0 - wide(first_rows))
    for t in range(NUM_HEADS // 2):
        two = jnp.concatenate([bias_ref[2 * t], bias_ref[2 * t + 1]], axis=1)
        bias_t[t // 2, pl.ds((t % 2) * LANES, LANES), :] = jnp.concatenate([two, two], axis=0).T

    gain_one = gain_one_ref[...]
    gain_two = gain_two_ref[...]

    def to_rows(recv, dest):
        tile = wide(recv[...])
        for half in range(2):
            mix[half] = tile[:, 8 * half : 8 * half + 8, :].reshape(LOCAL, LANES)
        for w in range(WINDOWS):
            for half in range(2):
                dest[pl.ds(w * AREA, AREA), pl.ds(half * LANES, LANES)] = mix[half, pl.ds(w, AREA, stride=WINDOWS), :]

    def from_rows(values, send):
        for w in range(WINDOWS):
            for half in range(2):
                mix[half, pl.ds(w, AREA, stride=WINDOWS), :] = values[
                    w * AREA : (w + 1) * AREA, half * LANES : (half + 1) * LANES
                ]
        send[...] = low(jnp.concatenate(
            [mix[0].reshape(AREA, WINDOWS, LANES), mix[1].reshape(AREA, WINDOWS, LANES)], axis=1
        ))

    loads[1].wait()
    cot_send[...] = pack_tile(wide(cot_ref[...]).reshape(AREA, WINDOWS, CHANNELS))
    exchange_start(cot_send, cot_recv, 1)

    exchange_recv(tok_recv, 0)
    to_rows(tok_recv, x_ref)
    normed_one, inverse_one = norm_forward(x_ref[...])
    n1_ref[...] = normed_one
    n1_low[...] = low(normed_one * gain_one)
    qkv_ref[...] = low(dot_nn(n1_low[...], wqkv_ref[...]))

    def block(ref, b, part, half):
        return ref[pl.ds(b * LANES, LANES), pl.ds(part * CHANNELS + half * LANES, LANES)]

    def spread(tile):
        return jnp.concatenate([jnp.concatenate([tile[:AREA]] * 4, axis=0) * head_mask,
                                jnp.concatenate([tile[AREA:]] * 4, axis=0) * head_mask], axis=1)

    def diagonal(tile):
        return jnp.concatenate([tile * top, tile * bottom], axis=1)

    def own_window(tile):
        return jnp.where(first_rows, tile[:, :LANES], tile[:, LANES:])

    def own_heads(tile):
        folded = jnp.sum((tile * head_wide).reshape(4, AREA, 2 * LANES), axis=0)
        return jnp.concatenate([folded[:, :LANES], folded[:, LANES:]], axis=0)

    order = [(b, half) for b in range(PAIRS) for half in range(2)]
    for b, half in order:
        slot = 2 * b + half
        kbig_ref[slot] = spread(block(qkv_ref, b, 1, half))
        vbig_ref[slot] = spread(block(qkv_ref, b, 2, half))
        scores = dot_nt(kbig_ref[slot], diagonal(block(qkv_ref, b, 0, half))) * SCORE_SCALE + bias_t[half]
        scores = scores.reshape(4, AREA, LANES)
        raised = jnp.exp(scores - jnp.max(scores, axis=1, keepdims=True))
        probs = raised * (1.0 / jnp.sum(raised, axis=1, keepdims=True))
        probs = probs.reshape(4 * AREA, LANES)
        probs_ref[slot] = probs
        mixed = dot_tn(low(probs), vbig_ref[slot])
        att_ref[pl.ds(b * LANES, LANES), pl.ds(half * LANES, LANES)] = low(own_window(mixed))
    branch = low(dot_nn(att_ref[...], wproj_ref[...]))
    mid_ref[...] = wide(low(x_ref[...] + wide(branch)))

    normed_two, inverse_two = norm_forward(mid_ref[...])
    n2_ref[...] = normed_two
    n2_low[...] = low(normed_two * gain_two)
    exchange_recv(cot_recv, 1)
    to_rows(cot_recv, cot_w)
    cot_low[...] = low(cot_w[...])
    n2_turned = low((normed_two * gain_two)).T
    for j in range(4):
        cut = pl.ds(j * 256, 256)
        preact = dot_nn(n2_low[...], fc1_ref[:, cut])
        activation, slope = gelu_parts(preact)
        activation = low(activation)
        grad_pre = low(dot_nt(cot_low[...], fc2_ref[cut, :]) * slope)
        out_term = dot_nn(activation, fc2_ref[cut, :])
        grad_term = dot_nt(grad_pre, fc1_ref[:, cut])
        if j == 0:
            acc_ref[...] = out_term
            gnm_ref[...] = grad_term
        else:
            acc_ref[...] += out_term
            gnm_ref[...] += grad_term
        block_b = low(dot_tn(activation, cot_low[...]))
        block_a = low(dot_nn(n2_turned, grad_pre))
        for r in range(4):
            for c in range(2):
                part_b[j // 2, ((j % 2) * 4 + r) * 2 + c, pl.ds(0, 64), :] = block_b[r * 64 : r * 64 + 64, c * LANES : (c + 1) * LANES]
                part_a[r // 2, (r % 2) * 8 + 2 * j + c] = block_a[r * 64 : r * 64 + 64, c * LANES : (c + 1) * LANES]
    core_start(parts[0])
    from_rows(wide(low(mid_ref[...] + acc_ref[...])), out_send)
    exchange_start(out_send, out_back, 2)

    gnm = gnm_ref[...]
    normed_two = n2_ref[...]
    gain_row_two = jnp.sum(gnm * normed_two, axis=0, keepdims=True)
    gm_low[...] = low(cot_w[...] + norm_backward(gnm, normed_two, inverse_two, gain_two))
    grad_proj = low(dot_tn(att_ref[...], gm_low[...]))
    for h in range(2):
        for r in range(8):
            for c in range(2):
                part_b[h, r * 2 + c, pl.ds(64, 16), :] = grad_proj[
                    h * 128 + r * 16 : h * 128 + r * 16 + 16, c * LANES : (c + 1) * LANES
                ]
    core_start(parts[1])
    gatt_ref[...] = low(dot_nt(gm_low[...], wproj_ref[...]))

    def put(ref, b, part, half, tile):
        ref[pl.ds(b * LANES, LANES), pl.ds(part * CHANNELS + half * LANES, LANES)] = low(tile)

    for n, (b, half) in enumerate(order):
        slot = 2 * b + half
        probs = probs_ref[slot]
        grad_diag = diagonal(block(gatt_ref, b, 0, half))
        grad_probs = dot_nt(vbig_ref[slot], grad_diag)
        put(gp_ref, b, 2, half, own_heads(dot_nn(low(probs), grad_diag)))
        weighted = (probs * grad_probs).reshape(4, AREA, LANES)
        total = jnp.sum(weighted, axis=1, keepdims=True)
        grad_scores = probs * (grad_probs.reshape(4, AREA, LANES) - total).reshape(4 * AREA, LANES)
        if b == 0:
            gbias[half] = grad_scores
        else:
            gbias[half] += grad_scores
        scores_low = low(grad_scores)
        put(gp_ref, b, 0, half, own_window(dot_tn(scores_low, kbig_ref[slot])) * SCORE_SCALE)
        query_diag = diagonal(block(qkv_ref, b, 0, half))
        put(gp_ref, b, 1, half, own_heads(dot_nn(scores_low, query_diag)) * SCORE_SCALE)
        if n == 2:
            plane_start(parts[0])
        if n == 4:
            plane_start(parts[1])

    grad_qkv = low(dot_tn(n1_low[...], gp_ref[...]))
    for h in range(2):
        for r in range(8):
            for c in range(6):
                part_c[h, r * 2 + c // 3, pl.ds((c % 3) * 16, 16), :] = grad_qkv[
                    h * 128 + r * 16 : h * 128 + r * 16 + 16, c * LANES : (c + 1) * LANES
                ]
    grad_normed_in = wide(low(dot_nt(gp_ref[...], wqkv_ref[...])))
    normed_one = n1_ref[...]
    gain_row_one = jnp.sum(grad_normed_in * normed_one, axis=0, keepdims=True)
    gains = jnp.concatenate(
        [gain_row_one[:, :LANES], gain_row_one[:, LANES:], gain_row_two[:, :LANES], gain_row_two[:, LANES:],
         jnp.zeros((4, LANES), F32)], axis=0,
    )
    for h in range(2):
        for t in range(2):
            tile = gbias[h, pl.ds(t * LANES, LANES), :]
            tile = (tile + pltpu.roll(tile, AREA, 1)).T
            for r in range(8):
                part_c[h, t * 8 + r, pl.ds(48, 16), :] = low(
                    jnp.concatenate([tile[8 * r : 8 * r + 8], gains], axis=0)
                )
    core_start(parts[2])
    grad_tokens = wide(gm_low[...]) + norm_backward(grad_normed_in, normed_one, inverse_one, gain_one)
    from_rows(wide(low(grad_tokens)), grad_send)

    plane_start(parts[2])
    exchange_start(grad_send, grad_back, 3)
    axis_start(parts[0])
    axis_start(parts[1])
    axis_start(parts[2])
    gather_start(parts[0])
    gather_start(parts[1])
    gather_start(parts[2])
    share_start(parts[0])
    share_start(parts[1])
    share_start(parts[2])
    exchange_recv(out_back, 2)
    exchange_recv(grad_back, 3)
    own_copy(out_send, out_back, 2).wait()
    own_copy(grad_send, grad_back, 3).wait()
    for k, send in enumerate((tok_send, cot_send, out_send, grad_send)):
        exchange_sent(send, k)
    for g in parts:
        share_wait(g)


def final_kernel(
    scale, out_back, grad_back, gath_a, gath_b, gath_c,
    out_ref, gtok_ref, gqkv_ref, gproj_ref, gbias_ref, gfc1_ref, gfc2_ref, gone_ref, gtwo_ref,
    *scratch,
):
    sources, (out_v, gtok_v, gqkv_v, gproj_v, gbias_v, gfc1_v, gfc2_v, gone_v, gtwo_v) = scratch[:5], scratch[5:14]
    load_sems, save_sems = scratch[14:]
    loads = [
        pltpu.make_async_copy(src, dst, load_sems.at[n])
        for n, (src, dst) in enumerate(zip((out_back, grad_back, gath_a, gath_b, gath_c), sources))
    ]
    for load in loads[2:] + loads[:2]:
        load.start()
    saves = [
        pltpu.make_async_copy(src, dst, save_sems.at[n])
        for n, (src, dst) in enumerate((
            (out_v, out_ref), (gtok_v, gtok_ref), (gfc1_v, gfc1_ref), (gfc2_v, gfc2_ref), (gproj_v, gproj_ref),
            (gqkv_v, gqkv_ref), (gbias_v, gbias_ref), (gone_v, gone_ref), (gtwo_v, gtwo_ref),
        ))
    ]
    halves = [(h, j) for h in range(2) for j in range(PIECES)]
    loads[2].wait()
    for h, j in halves:
        gfc1_v[pl.ds(h * 128 + (j // 8) * 64, 64), pl.ds((j % 8) * LANES, LANES)] = wide(sources[2][h, j]) * scale
    saves[2].start()
    loads[3].wait()
    for h, j in halves:
        tile = wide(sources[3][h, j]) * scale
        gfc2_v[pl.ds(h * 512 + (j // 2) * 64, 64), pl.ds((j % 2) * LANES, LANES)] = tile[:64]
        gproj_v[pl.ds(h * 128 + (j // 2) * 16, 16), pl.ds((j % 2) * LANES, LANES)] = tile[64:]
    saves[3].start()
    saves[4].start()
    loads[4].wait()
    for h, j in halves:
        tile = wide(sources[4][h, j]) * scale
        for c in range(3):
            gqkv_v[pl.ds(h * 128 + (j // 2) * 16, 16), pl.ds(((j % 2) * 3 + c) * LANES, LANES)] = (
                tile[16 * c : 16 * c + 16]
            )
        bias = tile[48:56] * AREA
        t, r = j // 8, j % 8
        gbias_v[4 * h + 2 * t, pl.ds(8 * r, 8), :] = bias[:, :AREA]
        gbias_v[4 * h + 2 * t + 1, pl.ds(8 * r, 8), :] = bias[:, AREA:]
        if h == 0 and j == 0:
            gone_v[:, :LANES] = tile[56:57]
            gone_v[:, LANES:] = tile[57:58]
            gtwo_v[:, :LANES] = tile[58:59]
            gtwo_v[:, LANES:] = tile[59:60]
    for save in saves[5:]:
        save.start()
    for n, dst in enumerate((out_v, gtok_v)):
        loads[n].wait()
        tile = wide(sources[n][...])
        joined = jnp.concatenate([tile[:, :8, :], tile[:, 8:, :]], axis=2)
        dst[...] = low(joined.reshape(dst.shape))
        saves[n].start()
    for save in saves:
        save.wait()


HBM = pl.BlockSpec(memory_space=pltpu.HBM)


def body(tokens, cotangent, gain_one, qkv_weight, proj_weight, rel_bias, gain_two, fc_one, fc_two):
    tile_rows, tile_cols, channels = tokens.shape
    total_tokens = tile_rows * tile_cols * lax.axis_size("row") * lax.axis_size("col")
    grad_scale = total_tokens ** (-0.5)

    def shape(*dims, dtype=BF16):
        return jax.ShapeDtypeStruct(dims, dtype)

    def vmem(*dims, dtype=BF16):
        return pltpu.VMEM(dims, dtype)

    swap = (AREA, 16, LANES)
    three = ((PIECES, 64, LANES), (PIECES, 80, LANES), (PIECES, 64, LANES))
    swapped = pl.pallas_call(
        fused_kernel,
        out_shape=(shape(*swap), shape(*swap), *[shape(2, *s) for s in three]),
        in_specs=[HBM] * 9,
        out_specs=(HBM,) * 5,
        scratch_shapes=[
            *[vmem(*swap) for _ in range(6)],
            *[vmem(2, *s) for s in three],
            *[vmem(*s) for s in three],
            *[vmem(*s) for s in three],
            *[vmem(*s) for s in three],
            *[vmem(4, *s[1:]) for s in three],
            *[vmem(*s[1:]) for s in three],
            vmem(2, LOCAL, LANES, dtype=F32),
            vmem(LOCAL, CHANNELS, dtype=F32),
            vmem(LOCAL, CHANNELS, dtype=F32),
            vmem(LOCAL, CHANNELS),
            vmem(LOCAL, CHANNELS, dtype=F32),
            vmem(LOCAL, CHANNELS),
            vmem(LOCAL, 3 * CHANNELS),
            vmem(LOCAL, CHANNELS),
            vmem(LOCAL, CHANNELS, dtype=F32),
            vmem(LOCAL, CHANNELS),
            vmem(LOCAL, CHANNELS, dtype=F32),
            vmem(LOCAL, CHANNELS, dtype=F32),
            vmem(LOCAL, CHANNELS, dtype=F32),
            vmem(LOCAL, CHANNELS),
            vmem(LOCAL, CHANNELS),
            vmem(LOCAL, 3 * CHANNELS),
            vmem(2, 4 * AREA, LANES, dtype=F32),
            vmem(2, 4 * AREA, LANES, dtype=F32),
            vmem(8, 4 * AREA, LANES, dtype=F32),
            vmem(8, 4 * AREA, 2 * LANES),
            vmem(8, 4 * AREA, 2 * LANES),
            vmem(*tokens.shape),
            vmem(*cotangent.shape),
            vmem(1, CHANNELS, dtype=F32),
            vmem(*qkv_weight.shape),
            vmem(*proj_weight.shape),
            vmem(*rel_bias.shape, dtype=F32),
            vmem(1, CHANNELS, dtype=F32),
            vmem(*fc_one.shape),
            vmem(*fc_two.shape),
            pltpu.SemaphoreType.DMA((46,)),
            pltpu.SemaphoreType.DMA((9,)),
        ],
        compiler_params=pltpu.CompilerParams(
            collective_id=0, has_side_effects=True, vmem_limit_bytes=60 * 1024 * 1024
        ),
        name="fused",
    )(
        tokens, cotangent, gain_one.reshape(1, -1), qkv_weight, proj_weight, rel_bias,
        gain_two.reshape(1, -1), fc_one, fc_two,
    )
    outs = (
        tokens.shape, tokens.shape, qkv_weight.shape, proj_weight.shape, rel_bias.shape, fc_one.shape, fc_two.shape,
        (1, CHANNELS), (1, CHANNELS),
    )
    types = (BF16, BF16, *[F32] * 7)
    results = pl.pallas_call(
        functools.partial(final_kernel, grad_scale),
        out_shape=tuple(shape(*dims, dtype=t) for dims, t in zip(outs, types)),
        in_specs=[HBM] * 5,
        out_specs=(HBM,) * 9,
        scratch_shapes=[
            vmem(*swap), vmem(*swap), *[vmem(2, *s) for s in three],
            *[vmem(*dims, dtype=t) for dims, t in zip(outs, types)],
            pltpu.SemaphoreType.DMA((5,)),
            pltpu.SemaphoreType.DMA((9,)),
        ],
        compiler_params=pltpu.CompilerParams(vmem_limit_bytes=60 * 1024 * 1024),
        name="finish",
    )(*swapped)
    return (*results[:7], results[7].reshape(-1), results[8].reshape(-1))


def solution(mesh):
    in_specs = (P("row", "col", None), P("row", "col", None), P(), P(), P(), P(), P(), P(), P())
    out_specs = (P("row", "col", None), P("row", "col", None), P(), P(), P(), P(), P(), P(), P())
    return jax.shard_map(body, mesh=mesh, in_specs=in_specs, out_specs=out_specs, check_vma=False)
```

```python
import functools

import jax
import jax.numpy as jnp
from jax import lax
from jax.experimental import pallas as pl
from jax.experimental.pallas import tpu as pltpu
from jax.sharding import PartitionSpec as P

NUM_HEADS = 8
HEAD_DIM = 32
GRID_SIDE = 8
AREA = GRID_SIDE * GRID_SIDE
CHANNELS = 256
MLP_DIM = 1024
WINDOWS = 8
LOCAL = WINDOWS * AREA
PAIRS = 4
LANES = 128
PIECES = 16

EPSILON = 1e-05
ROOT_HALF = 0.7071067811865476
DENSITY = 0.3989422804014327
SCORE_SCALE = HEAD_DIM ** (-0.5)

MESH = pl.DeviceIdType.MESH
BF16 = jnp.bfloat16
F32 = jnp.float32


def low(values):
    return values.astype(BF16)


def wide(values):
    return values.astype(F32)


def dot_nn(a, b):
    return lax.dot_general(a, b, (((1,), (0,)), ((), ())), preferred_element_type=F32)


def dot_nt(a, b):
    return lax.dot_general(a, b, (((1,), (1,)), ((), ())), preferred_element_type=F32)


def dot_tn(a, b):
    return lax.dot_general(a, b, (((0,), (0,)), ((), ())), preferred_element_type=F32)


def norm_forward(values):
    centre = jnp.mean(values, axis=-1, keepdims=True)
    shifted = values - centre
    spread = jnp.mean(shifted * shifted, axis=-1, keepdims=True)
    inverse = lax.rsqrt(spread + EPSILON)
    return (shifted * inverse, inverse)


def norm_backward(upstream, normed, inverse, gain_vec):
    scaled = upstream * gain_vec
    mean_first = jnp.mean(scaled, axis=-1, keepdims=True)
    second = jnp.mean(scaled * normed, axis=-1, keepdims=True)
    return inverse * (scaled - mean_first - normed * second)


def gelu_parts(preact):
    normal_cdf = 0.5 * (1.0 + lax.erf(preact * ROOT_HALF))
    return (preact * normal_cdf, normal_cdf + preact * DENSITY * jnp.exp(-0.5 * preact * preact))


def hops(steps):
    return sum(min(d, 4 - d) for d in steps)


PLANE_STEPS = sorted(((a, b) for a in range(4) for b in range(4) if a or b), key=hops, reverse=True)
CHIP_STEPS = sorted(
    ((a, b, c) for a in range(4) for b in range(4) for c in range(4) if a or b or c), key=hops, reverse=True
)


def pack_tile(tile):
    return low(jnp.concatenate([tile[:, :, :LANES], tile[:, :, LANES:]], axis=1))


def fused_kernel(
    tokens_in, cot_in, gain_one_in, wqkv_in, wproj_in, bias_in, gain_two_in, fc1_in, fc2_in,
    out_back, grad_back, gath_a, gath_b, gath_c,
    tok_send, cot_send, out_send, grad_send, tok_recv, cot_recv,
    part_a, part_b, part_c, crecv_a, crecv_b, crecv_c, psend_a, psend_b, psend_c,
    precv_a, precv_b, precv_c, axis_a, axis_b, axis_c, total_a, total_b, total_c,
    mix, x_ref, cot_w, cot_low, n1_ref, n1_low, qkv_ref, att_ref, n2_ref, n2_low, mid_ref,
    acc_ref, gnm_ref, gm_low, gatt_ref, gp_ref, bias_t, gbias, probs_ref, kbig_ref, vbig_ref,
    tokens_ref, cot_ref, gain_one_ref, wqkv_ref, wproj_ref, bias_ref, gain_two_ref, fc1_ref, fc2_ref,
    sems, load_sems,
):
    row, col = lax.axis_index("row"), lax.axis_index("col")
    core = col % 2
    me = row * GRID_SIDE + col // 2
    x, y, z = (row % 2) * 2 + (col // 2) % 2, row // 2, col // 4
    partner = (row, col + 1 - 2 * core)

    xs, ys, zs = ([(v + d) % 4 for d in range(4)] for v in (x, y, z))
    col_x, row_x = [v % 2 for v in xs], [v // 2 for v in xs]

    def device(dx, dy, dz):
        return (ys[dy] * 2 + row_x[dx], (zs[dz] * 2 + col_x[dx]) * 2 + core)

    peers = []
    for steps in CHIP_STEPS:
        peer_row, peer_col = device(*steps)
        peers.append((peer_row * GRID_SIDE + peer_col // 2, (peer_row, peer_col)))

    barrier = pltpu.get_barrier_semaphore()

    for _, peer in peers:
        pl.semaphore_signal(barrier, inc=1, device_id=peer, device_id_type=MESH)
    pl.semaphore_signal(barrier, inc=1, device_id=partner, device_id_type=MESH)

    loads = [
        pltpu.make_async_copy(src, dst, load_sems.at[n])
        for n, (src, dst) in enumerate((
            (tokens_in, tokens_ref), (cot_in, cot_ref), (gain_one_in, gain_one_ref), (wqkv_in, wqkv_ref),
            (bias_in, bias_ref), (wproj_in, wproj_ref), (gain_two_in, gain_two_ref), (fc1_in, fc1_ref),
            (fc2_in, fc2_ref),
        ))
    ]
    for load in loads:
        load.start()

    def exchange_start(send, recv, k):
        for p, peer in peers:
            remote(send.at[p], recv.at[me], 2 * k, peer).start()
        if k < 2:
            recv[me] = send[me]
        else:
            own_copy(send, recv, k).start()

    def own_copy(send, recv, k):
        return pltpu.make_async_copy(send.at[me], recv.at[me], sems.at[42 + k])

    def drain(ref, sem):
        pltpu.make_async_copy(ref, ref, sem).wait()

    def exchange_recv(recv, k):
        drain(recv.at[pl.ds(0, AREA - 1)], sems.at[2 * k + 1])

    def exchange_sent(send, k):
        drain(send.at[pl.ds(0, AREA - 1)], sems.at[2 * k])

    def plane_a(a, b):
        return (ys[a] * 4 + zs[b], device(0, a, b))

    def plane_b(a, b):
        return (zs[a] * 4 + xs[b], device(b, 0, a))

    def plane_c(a, b):
        return (ys[a] * 4 + xs[b], device(b, a, 0))

    parts = (
        (part_a, crecv_a, psend_a, precv_a, axis_a, total_a, gath_a, plane_a, y * 4 + z,
         lambda d: device(d, 0, 0), x, 8),
        (part_b, crecv_b, psend_b, precv_b, axis_b, total_b, gath_b, plane_b, z * 4 + x,
         lambda d: device(0, d, 0), y, 20),
        (part_c, crecv_c, psend_c, precv_c, axis_c, total_c, gath_c, plane_c, y * 4 + x,
         lambda d: device(0, 0, d), z, 32),
    )

    def remote(src, dst, k, device):
        return pltpu.make_async_remote_copy(
            src_ref=src, dst_ref=dst, send_sem=sems.at[k], recv_sem=sems.at[k + 1],
            device_id=device, device_id_type=MESH,
        )

    def core_start(g):
        part, crecv, _, _, _, _, _, _, _, _, _, k = g
        remote(part.at[1 - core], crecv, k, partner).start()

    def plane_start(g):
        part, crecv, psend, precv, _, _, _, where, mine, _, _, k = g
        drain(crecv, sems.at[k + 1])
        for steps in PLANE_STEPS:
            j, peer = where(*steps)
            psend[j] = low(wide(part[core, j]) + wide(crecv[j]))
            remote(psend.at[j], precv.at[mine], k + 2, peer).start()
        precv[mine] = low(wide(part[core, mine]) + wide(crecv[mine]))

    def axis_start(g):
        _, _, _, precv, axis, _, _, _, _, along, place, k = g
        drain(precv.at[pl.ds(0, PIECES - 1)], sems.at[k + 3])
        axis[place] = low(jnp.sum(wide(precv[...]), axis=0))
        for i in range(1, 4):
            remote(axis.at[place], axis.at[place], k + 4, along(i)).start()

    def gather_start(g):
        _, _, _, _, axis, held, _, where, mine, _, _, k = g
        drain(axis.at[pl.ds(0, 3)], sems.at[k + 5])
        held[mine] = low(jnp.sum(wide(axis[...]), axis=0))
        for steps in PLANE_STEPS:
            remote(held.at[mine], held.at[mine], k + 6, where(*steps)[1]).start()

    def held_copy(g):
        return pltpu.make_async_copy(g[5], g[6].at[core], sems.at[g[-1] + 10])

    def share_start(g):
        _, _, _, _, _, held, gath, _, _, _, _, k = g
        drain(held.at[pl.ds(0, PIECES - 1)], sems.at[k + 7])
        remote(held, gath.at[core], k + 8, partner).start()
        held_copy(g).start()

    def share_wait(g):
        part, crecv, psend, precv, axis, total, gath, _, _, _, _, k = g
        drain(gath.at[core], sems.at[k + 9])
        held_copy(g).wait()
        drain(crecv, sems.at[k])
        drain(psend.at[pl.ds(0, PIECES - 1)], sems.at[k + 2])
        drain(axis.at[pl.ds(0, 3)], sems.at[k + 4])
        drain(psend.at[pl.ds(0, PIECES - 1)], sems.at[k + 6])
        drain(crecv, sems.at[k + 8])

    loads[0].wait()
    tok_send[...] = pack_tile(wide(tokens_ref[...]).reshape(AREA, WINDOWS, CHANNELS))
    pl.semaphore_wait(barrier, AREA)
    exchange_start(tok_send, tok_recv, 0)
    for load in loads[2:]:
        load.wait()

    head_mask = low(wide(
        lax.broadcasted_iota(jnp.int32, (4 * AREA, LANES), 0) // AREA
        == lax.broadcasted_iota(jnp.int32, (4 * AREA, LANES), 1) // HEAD_DIM
    ))
    head_mask_two = jnp.concatenate([head_mask, head_mask], axis=1)
    head_wide = wide(head_mask_two)
    first_rows = lax.broadcasted_iota(jnp.int32, (LANES, LANES), 0) < AREA
    top = low(wide(first_rows))
    bottom = low(1.0 - wide(first_rows))
    for t in range(NUM_HEADS // 2):
        two = jnp.concatenate([bias_ref[2 * t], bias_ref[2 * t + 1]], axis=1)
        bias_t[t // 2, pl.ds((t % 2) * LANES, LANES), :] = jnp.concatenate([two, two], axis=0).T

    gain_one = gain_one_ref[...]
    gain_two = gain_two_ref[...]

    def to_rows(recv, dest):
        tile = wide(recv[...])
        for half in range(2):
            mix[half] = tile[:, 8 * half : 8 * half + 8, :].reshape(LOCAL, LANES)
        for w in range(WINDOWS):
            for half in range(2):
                dest[pl.ds(w * AREA, AREA), pl.ds(half * LANES, LANES)] = mix[half, pl.ds(w, AREA, stride=WINDOWS), :]

    def from_rows(values, send):
        for w in range(WINDOWS):
            for half in range(2):
                mix[half, pl.ds(w, AREA, stride=WINDOWS), :] = values[
                    w * AREA : (w + 1) * AREA, half * LANES : (half + 1) * LANES
                ]
        send[...] = low(jnp.concatenate(
            [mix[0].reshape(AREA, WINDOWS, LANES), mix[1].reshape(AREA, WINDOWS, LANES)], axis=1
        ))

    loads[1].wait()
    cot_send[...] = pack_tile(wide(cot_ref[...]).reshape(AREA, WINDOWS, CHANNELS))
    exchange_start(cot_send, cot_recv, 1)

    exchange_recv(tok_recv, 0)
    to_rows(tok_recv, x_ref)
    normed_one, inverse_one = norm_forward(x_ref[...])
    n1_ref[...] = normed_one
    n1_low[...] = low(normed_one * gain_one)
    qkv_ref[...] = low(dot_nn(n1_low[...], wqkv_ref[...]))

    def block(ref, b, part, half):
        return ref[pl.ds(b * LANES, LANES), pl.ds(part * CHANNELS + half * LANES, LANES)]

    def spread(tile):
        return jnp.concatenate([jnp.concatenate([tile[:AREA]] * 4, axis=0) * head_mask,
                                jnp.concatenate([tile[AREA:]] * 4, axis=0) * head_mask], axis=1)

    def diagonal(tile):
        return jnp.concatenate([tile * top, tile * bottom], axis=1)

    def own_window(tile):
        return jnp.where(first_rows, tile[:, :LANES], tile[:, LANES:])

    def own_heads(tile):
        folded = jnp.sum((tile * head_wide).reshape(4, AREA, 2 * LANES), axis=0)
        return jnp.concatenate([folded[:, :LANES], folded[:, LANES:]], axis=0)

    order = [(b, half) for b in range(PAIRS) for half in range(2)]
    for b, half in order:
        slot = 2 * b + half
        kbig_ref[slot] = spread(block(qkv_ref, b, 1, half))
        vbig_ref[slot] = spread(block(qkv_ref, b, 2, half))
        scores = dot_nt(kbig_ref[slot], diagonal(block(qkv_ref, b, 0, half))) * SCORE_SCALE + bias_t[half]
        scores = scores.reshape(4, AREA, LANES)
        raised = jnp.exp(scores - jnp.max(scores, axis=1, keepdims=True))
        probs = raised * (1.0 / jnp.sum(raised, axis=1, keepdims=True))
        probs = probs.reshape(4 * AREA, LANES)
        probs_ref[slot] = probs
        mixed = dot_tn(low(probs), vbig_ref[slot])
        att_ref[pl.ds(b * LANES, LANES), pl.ds(half * LANES, LANES)] = low(own_window(mixed))
    branch = low(dot_nn(att_ref[...], wproj_ref[...]))
    mid_ref[...] = wide(low(x_ref[...] + wide(branch)))

    normed_two, inverse_two = norm_forward(mid_ref[...])
    n2_ref[...] = normed_two
    n2_low[...] = low(normed_two * gain_two)
    exchange_recv(cot_recv, 1)
    to_rows(cot_recv, cot_w)
    cot_low[...] = low(cot_w[...])
    n2_turned = low((normed_two * gain_two)).T
    for j in range(4):
        cut = pl.ds(j * 256, 256)
        preact = dot_nn(n2_low[...], fc1_ref[:, cut])
        activation, slope = gelu_parts(preact)
        activation = low(activation)
        grad_pre = low(dot_nt(cot_low[...], fc2_ref[cut, :]) * slope)
        out_term = dot_nn(activation, fc2_ref[cut, :])
        grad_term = dot_nt(grad_pre, fc1_ref[:, cut])
        if j == 0:
            acc_ref[...] = out_term
            gnm_ref[...] = grad_term
        else:
            acc_ref[...] += out_term
            gnm_ref[...] += grad_term
        block_b = low(dot_tn(activation, cot_low[...]))
        block_a = low(dot_nn(n2_turned, grad_pre))
        for r in range(4):
            for c in range(2):
                part_b[j // 2, ((j % 2) * 4 + r) * 2 + c, pl.ds(0, 64), :] = block_b[r * 64 : r * 64 + 64, c * LANES : (c + 1) * LANES]
                part_a[r // 2, (r % 2) * 8 + 2 * j + c] = block_a[r * 64 : r * 64 + 64, c * LANES : (c + 1) * LANES]
    core_start(parts[0])
    from_rows(wide(low(mid_ref[...] + acc_ref[...])), out_send)
    exchange_start(out_send, out_back, 2)

    gnm = gnm_ref[...]
    normed_two = n2_ref[...]
    gain_row_two = jnp.sum(gnm * normed_two, axis=0, keepdims=True)
    gm_low[...] = low(cot_w[...] + norm_backward(gnm, normed_two, inverse_two, gain_two))
    grad_proj = low(dot_tn(att_ref[...], gm_low[...]))
    for h in range(2):
        for r in range(8):
            for c in range(2):
                part_b[h, r * 2 + c, pl.ds(64, 16), :] = grad_proj[
                    h * 128 + r * 16 : h * 128 + r * 16 + 16, c * LANES : (c + 1) * LANES
                ]
    core_start(parts[1])
    gatt_ref[...] = low(dot_nt(gm_low[...], wproj_ref[...]))

    def put(ref, b, part, half, tile):
        ref[pl.ds(b * LANES, LANES), pl.ds(part * CHANNELS + half * LANES, LANES)] = low(tile)

    for n, (b, half) in enumerate(order):
        slot = 2 * b + half
        probs = probs_ref[slot]
        grad_diag = diagonal(block(gatt_ref, b, 0, half))
        grad_probs = dot_nt(vbig_ref[slot], grad_diag)
        put(gp_ref, b, 2, half, own_heads(dot_nn(low(probs), grad_diag)))
        weighted = (probs * grad_probs).reshape(4, AREA, LANES)
        total = jnp.sum(weighted, axis=1, keepdims=True)
        grad_scores = probs * (grad_probs.reshape(4, AREA, LANES) - total).reshape(4 * AREA, LANES)
        if b == 0:
            gbias[half] = grad_scores
        else:
            gbias[half] += grad_scores
        scores_low = low(grad_scores)
        put(gp_ref, b, 0, half, own_window(dot_tn(scores_low, kbig_ref[slot])) * SCORE_SCALE)
        query_diag = diagonal(block(qkv_ref, b, 0, half))
        put(gp_ref, b, 1, half, own_heads(dot_nn(scores_low, query_diag)) * SCORE_SCALE)
        if n == 2:
            plane_start(parts[0])
        if n == 4:
            plane_start(parts[1])

    grad_qkv = low(dot_tn(n1_low[...], gp_ref[...]))
    for h in range(2):
        for r in range(8):
            for c in range(6):
                part_c[h, r * 2 + c // 3, pl.ds((c % 3) * 16, 16), :] = grad_qkv[
                    h * 128 + r * 16 : h * 128 + r * 16 + 16, c * LANES : (c + 1) * LANES
                ]
    grad_normed_in = wide(low(dot_nt(gp_ref[...], wqkv_ref[...])))
    normed_one = n1_ref[...]
    gain_row_one = jnp.sum(grad_normed_in * normed_one, axis=0, keepdims=True)
    gains = jnp.concatenate(
        [gain_row_one[:, :LANES], gain_row_one[:, LANES:], gain_row_two[:, :LANES], gain_row_two[:, LANES:],
         jnp.zeros((4, LANES), F32)], axis=0,
    )
    for h in range(2):
        for t in range(2):
            tile = gbias[h, pl.ds(t * LANES, LANES), :]
            tile = (tile + pltpu.roll(tile, AREA, 1)).T
            for r in range(8):
                part_c[h, t * 8 + r, pl.ds(48, 16), :] = low(
                    jnp.concatenate([tile[8 * r : 8 * r + 8], gains], axis=0)
                )
    core_start(parts[2])
    grad_tokens = wide(gm_low[...]) + norm_backward(grad_normed_in, normed_one, inverse_one, gain_one)
    from_rows(wide(low(grad_tokens)), grad_send)

    plane_start(parts[2])
    exchange_start(grad_send, grad_back, 3)
    axis_start(parts[0])
    axis_start(parts[1])
    axis_start(parts[2])
    gather_start(parts[0])
    gather_start(parts[1])
    gather_start(parts[2])
    share_start(parts[0])
    share_start(parts[1])
    share_start(parts[2])
    exchange_recv(out_back, 2)
    exchange_recv(grad_back, 3)
    own_copy(out_send, out_back, 2).wait()
    own_copy(grad_send, grad_back, 3).wait()
    for k, send in enumerate((tok_send, cot_send, out_send, grad_send)):
        exchange_sent(send, k)
    for g in parts:
        share_wait(g)


def final_kernel(
    scale, out_back, grad_back, gath_a, gath_b, gath_c,
    out_ref, gtok_ref, gqkv_ref, gproj_ref, gbias_ref, gfc1_ref, gfc2_ref, gone_ref, gtwo_ref,
    *scratch,
):
    sources, (out_v, gtok_v, gqkv_v, gproj_v, gbias_v, gfc1_v, gfc2_v, gone_v, gtwo_v) = scratch[:5], scratch[5:14]
    load_sems, save_sems = scratch[14:]
    loads = [
        pltpu.make_async_copy(src, dst, load_sems.at[n])
        for n, (src, dst) in enumerate(zip((out_back, grad_back, gath_a, gath_b, gath_c), sources))
    ]
    for load in loads[2:] + loads[:2]:
        load.start()
    saves = [
        pltpu.make_async_copy(src, dst, save_sems.at[n])
        for n, (src, dst) in enumerate((
            (out_v, out_ref), (gtok_v, gtok_ref), (gfc1_v, gfc1_ref), (gfc2_v, gfc2_ref), (gproj_v, gproj_ref),
            (gqkv_v, gqkv_ref), (gbias_v, gbias_ref), (gone_v, gone_ref), (gtwo_v, gtwo_ref),
        ))
    ]
    halves = [(h, j) for h in range(2) for j in range(PIECES)]
    loads[2].wait()
    for h, j in halves:
        gfc1_v[pl.ds(h * 128 + (j // 8) * 64, 64), pl.ds((j % 8) * LANES, LANES)] = wide(sources[2][h, j]) * scale
    saves[2].start()
    loads[3].wait()
    for h, j in halves:
        tile = wide(sources[3][h, j]) * scale
        gfc2_v[pl.ds(h * 512 + (j // 2) * 64, 64), pl.ds((j % 2) * LANES, LANES)] = tile[:64]
        gproj_v[pl.ds(h * 128 + (j // 2) * 16, 16), pl.ds((j % 2) * LANES, LANES)] = tile[64:]
    saves[3].start()
    saves[4].start()
    loads[4].wait()
    for h, j in halves:
        tile = wide(sources[4][h, j]) * scale
        for c in range(3):
            gqkv_v[pl.ds(h * 128 + (j // 2) * 16, 16), pl.ds(((j % 2) * 3 + c) * LANES, LANES)] = (
                tile[16 * c : 16 * c + 16]
            )
        bias = tile[48:56] * AREA
        t, r = j // 8, j % 8
        gbias_v[4 * h + 2 * t, pl.ds(8 * r, 8), :] = bias[:, :AREA]
        gbias_v[4 * h + 2 * t + 1, pl.ds(8 * r, 8), :] = bias[:, AREA:]
        if h == 0 and j == 0:
            gone_v[:, :LANES] = tile[56:57]
            gone_v[:, LANES:] = tile[57:58]
            gtwo_v[:, :LANES] = tile[58:59]
            gtwo_v[:, LANES:] = tile[59:60]
    for save in saves[5:]:
        save.start()
    for n, dst in enumerate((out_v, gtok_v)):
        loads[n].wait()
        tile = wide(sources[n][...])
        joined = jnp.concatenate([tile[:, :8, :], tile[:, 8:, :]], axis=2)
        dst[...] = low(joined.reshape(dst.shape))
        saves[n].start()
    for save in saves:
        save.wait()


HBM = pl.BlockSpec(memory_space=pltpu.HBM)


def body(tokens, cotangent, gain_one, qkv_weight, proj_weight, rel_bias, gain_two, fc_one, fc_two):
    tile_rows, tile_cols, channels = tokens.shape
    total_tokens = tile_rows * tile_cols * lax.axis_size("row") * lax.axis_size("col")
    grad_scale = total_tokens ** (-0.5)

    def shape(*dims, dtype=BF16):
        return jax.ShapeDtypeStruct(dims, dtype)

    def vmem(*dims, dtype=BF16):
        return pltpu.VMEM(dims, dtype)

    swap = (AREA, 16, LANES)
    three = ((PIECES, 64, LANES), (PIECES, 80, LANES), (PIECES, 64, LANES))
    swapped = pl.pallas_call(
        fused_kernel,
        out_shape=(shape(*swap), shape(*swap), *[shape(2, *s) for s in three]),
        in_specs=[HBM] * 9,
        out_specs=(HBM,) * 5,
        scratch_shapes=[
            *[vmem(*swap) for _ in range(6)],
            *[vmem(2, *s) for s in three],
            *[vmem(*s) for s in three],
            *[vmem(*s) for s in three],
            *[vmem(*s) for s in three],
            *[vmem(4, *s[1:]) for s in three],
            *[vmem(*s) for s in three],
            vmem(2, LOCAL, LANES, dtype=F32),
            vmem(LOCAL, CHANNELS, dtype=F32),
            vmem(LOCAL, CHANNELS, dtype=F32),
            vmem(LOCAL, CHANNELS),
            vmem(LOCAL, CHANNELS, dtype=F32),
            vmem(LOCAL, CHANNELS),
            vmem(LOCAL, 3 * CHANNELS),
            vmem(LOCAL, CHANNELS),
            vmem(LOCAL, CHANNELS, dtype=F32),
            vmem(LOCAL, CHANNELS),
            vmem(LOCAL, CHANNELS, dtype=F32),
            vmem(LOCAL, CHANNELS, dtype=F32),
            vmem(LOCAL, CHANNELS, dtype=F32),
            vmem(LOCAL, CHANNELS),
            vmem(LOCAL, CHANNELS),
            vmem(LOCAL, 3 * CHANNELS),
            vmem(2, 4 * AREA, LANES, dtype=F32),
            vmem(2, 4 * AREA, LANES, dtype=F32),
            vmem(8, 4 * AREA, LANES, dtype=F32),
            vmem(8, 4 * AREA, 2 * LANES),
            vmem(8, 4 * AREA, 2 * LANES),
            vmem(*tokens.shape),
            vmem(*cotangent.shape),
            vmem(1, CHANNELS, dtype=F32),
            vmem(*qkv_weight.shape),
            vmem(*proj_weight.shape),
            vmem(*rel_bias.shape, dtype=F32),
            vmem(1, CHANNELS, dtype=F32),
            vmem(*fc_one.shape),
            vmem(*fc_two.shape),
            pltpu.SemaphoreType.DMA((46,)),
            pltpu.SemaphoreType.DMA((9,)),
        ],
        compiler_params=pltpu.CompilerParams(
            collective_id=0, has_side_effects=True, vmem_limit_bytes=60 * 1024 * 1024
        ),
        name="fused",
    )(
        tokens, cotangent, gain_one.reshape(1, -1), qkv_weight, proj_weight, rel_bias,
        gain_two.reshape(1, -1), fc_one, fc_two,
    )
    outs = (
        tokens.shape, tokens.shape, qkv_weight.shape, proj_weight.shape, rel_bias.shape, fc_one.shape, fc_two.shape,
        (1, CHANNELS), (1, CHANNELS),
    )
    types = (BF16, BF16, *[F32] * 7)
    results = pl.pallas_call(
        functools.partial(final_kernel, grad_scale),
        out_shape=tuple(shape(*dims, dtype=t) for dims, t in zip(outs, types)),
        in_specs=[HBM] * 5,
        out_specs=(HBM,) * 9,
        scratch_shapes=[
            vmem(*swap), vmem(*swap), *[vmem(2, *s) for s in three],
            *[vmem(*dims, dtype=t) for dims, t in zip(outs, types)],
            pltpu.SemaphoreType.DMA((5,)),
            pltpu.SemaphoreType.DMA((9,)),
        ],
        compiler_params=pltpu.CompilerParams(vmem_limit_bytes=60 * 1024 * 1024),
        name="finish",
    )(*swapped)
    return (*results[:7], results[7].reshape(-1), results[8].reshape(-1))


def solution(mesh):
    in_specs = (P("row", "col", None), P("row", "col", None), P(), P(), P(), P(), P(), P(), P())
    out_specs = (P("row", "col", None), P("row", "col", None), P(), P(), P(), P(), P(), P(), P())
    return jax.shard_map(body, mesh=mesh, in_specs=in_specs, out_specs=out_specs, check_vma=False)
```
